512 devices in a mesh: gy: 16 (over z_hi, y), gz: 4 (over z_lo), band: 8 (over x, core).
Axes of the slice: x: 4, y: 8, z: 8 (z_hi: 2, z_lo: 4; z = z_hi * 4 + z_lo), core: 2. Of those that a mesh axis runs over, the one named last changes fastest.
Arguments:
- previous: float32 [128, 128, 32, 128], P('band', 'gy', 'gz'), may hold values from -2.4 to 2.4
- current: float32 [128, 128, 32, 128], P('band', 'gy', 'gz'), may hold values from 0.5 to 4.5
- potential: float32 [128, 32, 128], P('gy', 'gz'), may hold values from 0 to 2
- projectors: float32 [64, 128, 32, 128], P(None, 'gy', 'gz'), may hold values from -0.0625 to 0.0625
- couplings: float32 [64], replicated, may hold values from 0.5 to 2
- pattern: int32 [8, 64], replicated, may hold values 0 or 1
- counts: int32 [8], replicated, may hold values from 1 to 8, as said below
- panels: float32 [256, 128, 32, 128], P('band', 'gy', 'gz'), may hold values from -0.03125 to 0.03125
Outputs:
- rotated: float32 [128, 128, 32, 128], P('band', 'gy', 'gz')
- coefficients: float32 [256, 128], P(None, 'band')
The draws below stay inside these ranges and needn't reach their ends.
Inputs may be any that keep to these rules, and one draw needn't show every extreme that they name: `counts`: some atom block has all 8 slots live.
All inputs are finite; a program needn't handle non-finite values.
Results may differ from the reference program's by a relative error of at most 0.00011.
Values sent between devices are 32-bit elements; how exact they have to be, the bound alone decides.
A program may use at most 128 MiB of HBM per device.

```python
import math
import jax
import jax.numpy as jnp
from jax import lax

PANELS = 256
NX = 128
CY = 8
CZ = 8
NBLK = 8
PB = 8
NPR = 64
TILES = 64
NB = 128
NY = 128
NZ = 32
N_GY = 16
N_GZ = 4


def draw_counts(key, part):
    first_key, second_key = jax.random.split(jax.random.fold_in(key, 17))
    values_drawn = jax.random.randint(first_key, (NBLK,), 1, PB + 1)
    full_block = jax.random.randint(second_key, (), 0, NBLK)
    return jnp.where(jnp.arange(NBLK) == full_block, PB, values_drawn).astype(jnp.int32)


def draw_current(key, part):
    rough_key = jax.random.fold_in(jax.random.fold_in(key, 23), 1)
    rough = jax.random.truncated_normal(rough_key, -4.0, 4.0, (NB, NY, NZ, NX), jnp.float32)
    return (2.5 + 0.4 * rough).astype(jnp.float32)


def plant(array, own_key, least, high):
    dims = array.shape
    index_at = [jax.random.randint(jax.random.fold_in(own_key, axis), (), 0, dims[axis]) for axis in range(len(dims))]
    array = array.at[tuple(index_at)].set(least)
    longest = dims.index(max(dims))
    index_at[longest] = (index_at[longest] + 1) % dims[longest]
    return array.at[tuple(index_at)].set(high)


def block_levels(stream_key, dims, shards, least, top_value):
    factor_of = 1.0
    for axis_at, parts in shards:
        steps = jax.random.uniform(jax.random.fold_in(jax.random.fold_in(stream_key, 6), axis_at), (parts,), jnp.float32, least / len(shards), top_value / len(shards))
        factor_of = factor_of * jnp.repeat(jnp.exp(steps), dims[axis_at] // parts).reshape((-1,) + (1,) * (len(dims) - 1 - axis_at))
    return factor_of


def centred(key, shape, deviation, most, shards=(), kind=jnp.bfloat16):
    loudness = block_levels(key, shape, shards, -0.22, 0.18) if shards else 1.0
    entries = jax.random.normal(key, shape, jnp.float32) * deviation * loudness
    return jnp.minimum(jnp.maximum(entries, -most), most).astype(kind)


def setup_inputs(seed: int = 0) -> dict:
    key_of = jax.random.split(jax.random.key(seed), 9)
    previous = centred(key_of[0], (NB, NY, NZ, NX), 0.3, 2.4, ((0, 8), (1, 16), (2, 4)), jnp.float32)
    current = draw_current(jax.random.fold_in(key_of[8], 71), 0)
    potential = jnp.clip(2.0 * jax.random.uniform(key_of[2], (NY, NZ, NX), jnp.float32) ** block_levels(key_of[2], (NY, NZ, NX), ((0, 16), (1, 4)), -0.2, 0.2), 0.0, 2.0)
    projectors = centred(key_of[3], (NPR, NY, NZ, NX), (NY * NZ * NX // 64) ** -0.5, 0.0625, ((1, 16), (2, 4)), jnp.float32)
    couplings = jnp.clip(jnp.exp(jax.random.uniform(key_of[4], (NPR,), jnp.float32, math.log(0.5), math.log(2.0))), 0.5, 2.0)
    pattern = plant((jax.random.randint(key_of[5], (NBLK, TILES), 0, 2) < 1).astype(jnp.int32), jax.random.fold_in(key_of[5], 1), 0, 1)
    counts = draw_counts(jax.random.fold_in(key_of[8], 71), 0)
    panels = centred(key_of[7], (PANELS, NY, NZ, NX), (NY * NZ * NX // 16) ** -0.5, 0.03125, ((0, 8), (1, 16), (2, 4)), jnp.float32)
    return dict(previous=previous, current=current, potential=potential, projectors=projectors, couplings=couplings, pattern=pattern, counts=counts, panels=panels)


STENCIL = (-5369.0 / 1800.0, 12.0 / 7.0, -15.0 / 56.0, 10.0 / 189.0, -1.0 / 112.0, 2.0 / 1925.0, -1.0 / 16632.0)
CENTER = 1.0
HALF_WIDTH = 5.0


def laplace(values_in):
    result = 3.0 * STENCIL[0] * values_in
    for reach in range(1, 7):
        for which in (0, 1, 2):
            result = result + STENCIL[reach] * (jnp.roll(values_in, reach, which) + jnp.roll(values_in, -reach, which))
    return result


def reference(previous, current, potential, projectors, couplings, pattern, counts, panels):
    cell_count = NY * NZ * NX
    tile_live = pattern.reshape(NBLK, N_GY, N_GZ).astype(jnp.float32)
    tile_live = jnp.repeat(jnp.repeat(tile_live, CY, axis=1), CZ, axis=2)
    slot_live = (jnp.arange(PB, dtype=jnp.int32)[None, :] < counts[:, None]).astype(jnp.float32)
    weights = slot_live[:, :, None, None, None] * tile_live[:, None, :, :, None]
    effective = (projectors.reshape(NBLK, PB, NY, NZ, NX) * weights).reshape(NPR, cell_count)

    def local_step(pair_of):
        earlier, present = pair_of
        return (2.0 / HALF_WIDTH) * (-0.5 * laplace(present) + potential * present - CENTER * present) - earlier

    partial_block = lax.map(local_step, (previous, current))
    flat_block = current.reshape(NB, cell_count)
    proj_sums = jnp.dot(effective, flat_block.T, precision=lax.Precision.HIGHEST, preferred_element_type=jnp.float32)
    projected = jnp.dot((couplings[:, None] * proj_sums).T, effective, precision=lax.Precision.HIGHEST, preferred_element_type=jnp.float32)
    filtered = partial_block.reshape(NB, cell_count) + (2.0 / HALF_WIDTH) * projected
    panel_rows = panels.reshape(PANELS, cell_count)
    coefficients = jnp.dot(panel_rows, filtered.T, precision=lax.Precision.HIGHEST, preferred_element_type=jnp.float32)
    rotated = filtered - jnp.dot(coefficients.T, panel_rows, precision=lax.Precision.HIGHEST, preferred_element_type=jnp.float32)
    return rotated.reshape(NB, NY, NZ, NX), coefficients
```

```python
import jax
import jax.numpy as jnp
from jax import lax
from jax.experimental import pallas as pl
from jax.experimental.pallas import tpu as pltpu
from jax.sharding import PartitionSpec as P

STENCIL = (
    -5369.0 / 1800.0,
    12.0 / 7.0,
    -15.0 / 56.0,
    10.0 / 189.0,
    -1.0 / 112.0,
    2.0 / 1925.0,
    -1.0 / 16632.0,
)
CENTER = 1.0
HALF_WIDTH = 5.0
SCALE = 2.0 / HALF_WIDTH

N = 16
C = 8
X = 128
NPR = 64
SHARD = 32
NP = 256
CHUNK = 8
F32 = jnp.float32
BF16 = jnp.bfloat16
MESH = pl.DeviceIdType.MESH
ANY = pl.BlockSpec(memory_space=pl.ANY)
SMEM = pl.BlockSpec(memory_space=pltpu.SMEM)


def split(value):
    high = value.astype(BF16)
    return high, (value - high.astype(F32)).astype(BF16)


def same_layer(rows, columns):
    row = lax.broadcasted_iota(jnp.int32, (rows, columns), 0)
    column = lax.broadcasted_iota(jnp.int32, (rows, columns), 1)
    return (row & 7) == (column & 7)


def dot(left, right):
    return jnp.dot(left, right, preferred_element_type=F32)


def convert(source, target, first, count):
    @pl.loop(0, count // 16)
    def _(step):
        start = pl.multiple_of(first + step * 16, 8)
        row = pl.multiple_of(start * 8, 64)
        for y in range(C):
            rows = source[pl.ds(start, 16), y * 8 : y * 8 + 8, :].reshape(128, X)
            high, low = split(rows)
            target[pl.ds(row, 128), y * X : (y + 1) * X] = high
            target[pl.ds(row, 128), (C + y) * X : (C + y + 1) * X] = low


def transpose_block(source, target):
    for y in range(C):
        rows = source[:, y * 8 : y * 8 + 8, :].reshape(N * 8, X).T
        high, low = split(rows)
        target[y * X : (y + 1) * X, 0:128] = high
        target[y * X : (y + 1) * X, 128:256] = low


def contract(table, block, sums, first, count):
    @pl.loop(0, count // 32)
    def _(step):
        start = pl.multiple_of(first + step * 32, 32)
        rows = pl.ds(pl.multiple_of(start * 8, 256), 256)
        full = dot(table[rows, 0:1024], block[...]) + dot(table[rows, 1024:2048], block[...])
        both = full[:, 0:128] + full[:, 128:256]
        kept = jnp.where(same_layer(256, 128), both, 0.0)
        sums[pl.ds(start, 32), :] = kept.reshape(32, 8, 128).sum(axis=1)


def fold_layers(sums):
    band = lax.broadcasted_iota(jnp.int32, (N, 128), 0)
    column = lax.broadcasted_iota(jnp.int32, (N, 128), 1)
    ones = jnp.where(band == (column >> 3), 1.0, 0.0).astype(F32)
    return lax.dot_general(
        ones,
        sums,
        (((1,), (1,)), ((), ())),
        precision=lax.Precision.HIGHEST,
        preferred_element_type=F32,
    )


def spread(coefs, repeat, target, columns):
    count = coefs.shape[1]
    wide = jnp.broadcast_to(coefs[:, None, :], (N, 8, count)).reshape(N * 8, count)
    high, low = split(wide)
    both = jnp.concatenate([high, low], axis=0)
    for at in range(0, columns, 256):
        values = dot(both, repeat[0:count, at : at + 256])
        target[:, at : at + 256] = jnp.where(same_layer(256, 256), values, 0.0).astype(BF16)


def kernel(
    prev_hbm, cur_hbm, pot_hbm, proj_hbm, coup, pattern, counts, pan_hbm,
    out_hbm, coef_out,
    cur, turned, y_low, y_high, z_low, z_high, filt, prev, pot, proj, proj_split,
    gathered, pan_split, block, repeat, spread_ref, sums, small_a, small_b, coef_a, coef_b,
    load_sem, halo_send, halo_recv, right_send, left_recv, left_send, right_recv,
    sib_send, sib_recv, ahead_send, behind_recv, back_send, front_recv,
    sum_send, sum_recv, store_sem,
):
    gy, gz, band = lax.axis_index("gy"), lax.axis_index("gz"), lax.axis_index("band")
    z_hi, y = gy // 8, gy % 8
    z = z_hi * 4 + gz
    x, core = band // 2, band % 2

    def at_y(other):
        return {"gy": z_hi * 8 + other, "gz": gz, "band": band}

    def at_z(other):
        return {"gy": (other // 4) * 8 + y, "gz": other % 4, "band": band}

    def at_band(other):
        return {"gy": gy, "gz": gz, "band": other}

    up_y = {"gy": (gy + 1) % 16, "gz": gz, "band": band}
    down_y = {"gy": (gy + 15) % 16, "gz": gz, "band": band}
    up_z = {"gy": gy, "gz": (gz + 1) % 4, "band": band}
    down_z = {"gy": gy, "gz": (gz + 3) % 4, "band": band}
    right, left = ((x + 1) % 4) * 2 + core, ((x + 3) % 4) * 2 + core
    opposite, sibling = ((x + 2) % 4) * 2 + core, x * 2 + 1 - core

    own_rows = pl.ds(pl.multiple_of(band * SHARD, SHARD), SHARD)
    load_pan = pltpu.make_async_copy(pan_hbm, gathered.at[own_rows], load_sem.at[0])
    load_cur = pltpu.make_async_copy(cur_hbm, cur, load_sem.at[1])
    load_proj = pltpu.make_async_copy(proj_hbm, proj, load_sem.at[2])
    load_prev = pltpu.make_async_copy(prev_hbm, prev, load_sem.at[3])
    load_pot = pltpu.make_async_copy(pot_hbm, pot, load_sem.at[4])
    for load in (load_pan, load_cur, load_proj, load_prev, load_pot):
        load.start()

    barrier = pltpu.get_barrier_semaphore()
    partners = [at_y((y + r) % 8) for r in range(1, 8)]
    partners += [at_z((z + r) % 8) for r in range(1, 8)]
    partners += [up_y, down_y, up_z, down_z]
    partners += [at_band(right), at_band(left), at_band(sibling)]
    for partner in partners:
        pl.semaphore_signal(barrier, inc=1, device_id=partner, device_id_type=MESH)
    pl.semaphore_wait(barrier, len(partners))

    def remote(source, target, send, recv, device):
        return pltpu.make_async_remote_copy(
            src_ref=source, dst_ref=target, send_sem=send, recv_sem=recv,
            device_id=device, device_id_type=MESH,
        )

    def panel_copy(owner, k, send, recv, device):
        rows = gathered.at[pl.ds(pl.multiple_of(owner * SHARD + k * CHUNK, CHUNK), CHUNK)]
        return remote(rows, rows, send, recv, device)

    load_pan.wait()
    started = []
    for step in range(4):
        k = step
        started.append(panel_copy(band, k, right_send.at[k], left_recv.at[k], at_band(right)))
        started[-1].start()
        k = (step + 2) % 4
        started.append(panel_copy(band, k, left_send.at[k], right_recv.at[k], at_band(left)))
        started[-1].start()
    for k in range(4):
        started.append(panel_copy(band, k, sib_send.at[k], sib_recv.at[k], at_band(sibling)))
        started[-1].start()

    load_cur.wait()
    halo_y0 = remote(cur.at[:, pl.ds(16, 48)], y_low, halo_send.at[0], halo_recv.at[0], up_y)
    halo_y1 = remote(cur.at[:, pl.ds(0, 48)], y_high, halo_send.at[1], halo_recv.at[1], down_y)
    halo_y0.start()
    halo_y1.start()

    @pl.loop(0, N)
    def _(n):
        for layer in range(C):
            turned[n, layer * 8 : layer * 8 + 8, :] = cur[n, pl.ds(layer, 8, stride=8), :]

    halo_z0 = remote(turned.at[:, pl.ds(16, 48)], z_low, halo_send.at[2], halo_recv.at[2], up_z)
    halo_z1 = remote(turned.at[:, pl.ds(0, 48)], z_high, halo_send.at[3], halo_recv.at[3], down_z)
    halo_z0.start()
    halo_z1.start()

    transpose_block(cur, block)
    load_proj.wait()
    convert(proj, proj_split, 0, NPR)
    contract(proj_split, block, sums, 0, NPR)
    sums[NPR:128, :] = jnp.zeros((128 - NPR, 128), F32)

    lane = lax.broadcasted_iota(jnp.int32, (N, 128), 1)
    tile = gy * 4 + gz
    weight = jnp.zeros((N, 128), F32)
    for b in range(8):
        reached = pattern[b, tile].astype(F32)
        live = ((lane >> 3) == b) & ((lane & 7) < counts[b])
        weight = jnp.where(live, reached, weight)
    coupling = jnp.zeros((N, 128), F32)
    for j in range(NPR):
        coupling = jnp.where(lane == j, coup[j], coupling)

    def send_y(buffer, sems):
        copies = []
        for r in range(1, 8):
            copies.append(
                remote(buffer.at[y], buffer.at[y], sum_send.at[sems, r], sum_recv.at[sems, y], at_y((y + r) % 8))
            )
            copies[-1].start()
        return copies

    def send_z(buffer, sems):
        copies = []
        for r in range(1, 8):
            copies.append(
                remote(buffer.at[z], buffer.at[z], sum_send.at[sems, r], sum_recv.at[sems, z], at_z((z + r) % 8))
            )
            copies[-1].start()
        return copies

    def receive(buffer, sems, me):
        for r in range(1, 8):
            other = (me + r) % 8
            remote(buffer.at[other], buffer.at[other], sum_send.at[sems, r], sum_recv.at[sems, other], up_y).wait_recv()

    def total(buffer):
        value = buffer[0]
        for i in range(1, 8):
            value = value + buffer[i]
        return value

    small_a[y] = fold_layers(sums[0:128, :]) * weight
    sent = send_y(small_a, 0)

    load_prev.wait()
    load_pot.wait()

    @pl.loop(0, N)
    def _(n):
        value = cur[n]
        lap = 3.0 * STENCIL[0] * value
        for reach in range(1, 7):
            lap = lap + STENCIL[reach] * (pltpu.roll(value, reach, 1) + pltpu.roll(value, X - reach, 1))
        filt[n] = SCALE * (-0.5 * lap + pot[...] * value - CENTER * value) - prev[n]

    receive(small_a, 0, y)
    small_b[z] = total(small_a)
    sent += send_z(small_b, 1)

    @pl.loop(0, 8)
    def _(step):
        at = pl.multiple_of(step * 256, 256)
        row = lax.broadcasted_iota(jnp.int32, (NP, 256), 0)
        column = lax.broadcasted_iota(jnp.int32, (NP, 256), 1) + at
        repeat[:, pl.ds(at, 256)] = jnp.where(row == (column >> 3), 1.0, 0.0).astype(BF16)

    own_first = pl.multiple_of(band * SHARD, SHARD)
    convert(gathered, pan_split, own_first, SHARD)

    receive(small_b, 1, z)
    spread(total(small_b) * (coupling * weight), repeat, spread_ref, 512)
    for part in range(4):
        at = part * 256
        value = dot(spread_ref[:, 0:512], proj_split[:, at : at + 256])
        value = value[0:128] + value[128:256] + dot(spread_ref[0:128, 0:512], proj_split[:, 1024 + at : 1280 + at])
        for half in range(2):
            rows = pl.ds((part * 2 + half) * 8, 8)
            filt[:, rows, :] += SCALE * value[:, half * X : (half + 1) * X].reshape(N, 8, X)

    def pass_on(copy):
        copy.start()
        started.append(copy)

    for step in range(4):
        k = step
        panel_copy(left, k, right_send.at[k], left_recv.at[k], at_band(right)).wait_recv()
        if k < 2:
            pass_on(panel_copy(left, k, ahead_send.at[k], behind_recv.at[k], at_band(right)))
        pass_on(panel_copy(left, k, sib_send.at[4 + k], sib_recv.at[4 + k], at_band(sibling)))
        k = (step + 2) % 4
        panel_copy(right, k, left_send.at[k], right_recv.at[k], at_band(left)).wait_recv()
        if k >= 2:
            pass_on(panel_copy(right, k, back_send.at[k - 2], front_recv.at[k - 2], at_band(left)))
        pass_on(panel_copy(right, k, sib_send.at[8 + k], sib_recv.at[8 + k], at_band(sibling)))

    def take(owner, slot):
        for k in range(4):
            panel_copy(owner, k, sib_send.at[slot + k], sib_recv.at[slot + k], at_band(sibling)).wait_recv()

    def other_core(owner):
        return owner + 1 - 2 * core

    def convert_shard(owner):
        convert(gathered, pan_split, pl.multiple_of(owner * SHARD, SHARD), SHARD)

    take(sibling, 0)
    convert_shard(sibling)
    convert_shard(left)
    convert_shard(right)
    take(other_core(left), 4)
    convert_shard(other_core(left))
    take(other_core(right), 8)
    convert_shard(other_core(right))

    halo_y0.wait_recv()
    halo_y1.wait_recv()

    def stencil(rows):
        result = []
        for at in range(C):
            value = None
            for reach in range(1, 7):
                pair = STENCIL[reach] * (rows[6 + at + reach] + rows[6 + at - reach])
                value = pair if value is None else value + pair
            result.append(-0.5 * SCALE * value)
        return result

    def lines(ref, n, count):
        return [ref[n, i * 8 : i * 8 + 8, :] for i in range(count)]

    @pl.loop(0, N)
    def _(n):
        parts = stencil(lines(y_low, n, 6) + lines(cur, n, 8) + lines(y_high, n, 6))
        for at in range(C):
            filt[n, at * 8 : at * 8 + 8, :] += parts[at]

    halo_z0.wait_recv()
    halo_z1.wait_recv()

    @pl.loop(0, N)
    def _(n):
        parts = stencil(lines(z_low, n, 6) + lines(turned, n, 8) + lines(z_high, n, 6))
        for at in range(C):
            filt[n, pl.ds(at, 8, stride=8), :] += parts[at]

    transpose_block(filt, block)

    for k in (0, 1):
        panel_copy(opposite, k, ahead_send.at[k], behind_recv.at[k], at_band(right)).wait_recv()
        pass_on(panel_copy(opposite, k, sib_send.at[12 + k], sib_recv.at[12 + k], at_band(sibling)))
        panel_copy(opposite, k + 2, back_send.at[k], front_recv.at[k], at_band(left)).wait_recv()
        pass_on(panel_copy(opposite, k + 2, sib_send.at[14 + k], sib_recv.at[14 + k], at_band(sibling)))
    convert_shard(opposite)
    take(other_core(opposite), 12)
    convert_shard(other_core(opposite))

    contract(pan_split, block, sums, 0, NP)
    coef_a[y] = fold_layers(sums[...])
    sent += send_y(coef_a, 2)
    receive(coef_a, 2, y)
    coef_b[z] = total(coef_a)
    sent += send_z(coef_b, 3)
    receive(coef_b, 3, z)
    coefs = total(coef_b)
    coef_out[...] = coefs
    spread(coefs, repeat, spread_ref, 2048)
    stores = []
    for part in range(4):
        at = part * 256
        value = dot(spread_ref[...], pan_split[:, at : at + 256])
        value = value[0:128] + value[128:256] + dot(spread_ref[0:128, :], pan_split[:, 1024 + at : 1280 + at])
        for half in range(2):
            rows = pl.ds((part * 2 + half) * 8, 8)
            filt[:, rows, :] -= value[:, half * X : (half + 1) * X].reshape(N, 8, X)
        rows = pl.ds(part * 16, 16)
        stores.append(pltpu.make_async_copy(filt.at[:, rows], out_hbm.at[:, rows], store_sem.at[part]))
        stores[-1].start()

    for copy in started + sent + [halo_y0, halo_y1, halo_z0, halo_z1]:
        copy.wait_send()
    for copy in stores:
        copy.wait()


def per_device(previous, current, potential, projectors, couplings, pattern, counts, panels):
    rows = C * C
    vmem = pltpu.VMEM
    dma = pltpu.SemaphoreType.DMA
    rotated, coefs = pl.pallas_call(
        kernel,
        out_shape=(
            jax.ShapeDtypeStruct((N, rows, X), F32),
            jax.ShapeDtypeStruct((N, NP), F32),
        ),
        in_specs=[ANY, ANY, ANY, ANY, SMEM, SMEM, SMEM, ANY],
        out_specs=(ANY, pl.BlockSpec(memory_space=pltpu.VMEM)),
        scratch_shapes=[
            vmem((N, rows, X), F32),
            vmem((N, rows, X), F32),
            vmem((N, 48, X), F32),
            vmem((N, 48, X), F32),
            vmem((N, 48, X), F32),
            vmem((N, 48, X), F32),
            vmem((N, rows, X), F32),
            vmem((N, rows, X), F32),
            vmem((rows, X), F32),
            vmem((NPR, rows, X), F32),
            vmem((NPR * 8, 2048), BF16),
            vmem((NP, rows, X), F32),
            vmem((NP * 8, 2048), BF16),
            vmem((1024, 256), BF16),
            vmem((NP, 2048), BF16),
            vmem((256, 2048), BF16),
            vmem((NP, 128), F32),
            vmem((8, N, 128), F32),
            vmem((8, N, 128), F32),
            vmem((8, N, NP), F32),
            vmem((8, N, NP), F32),
            dma((5,)),
            dma((4,)),
            dma((4,)),
            dma((4,)),
            dma((4,)),
            dma((4,)),
            dma((4,)),
            dma((16,)),
            dma((16,)),
            dma((2,)),
            dma((2,)),
            dma((2,)),
            dma((2,)),
            dma((4, 8)),
            dma((4, 8)),
            dma((4,)),
        ],
        compiler_params=pltpu.CompilerParams(
            collective_id=0, has_side_effects=True, vmem_limit_bytes=56 * 1024 * 1024
        ),
        cost_estimate=pl.CostEstimate(flops=10**9, bytes_accessed=5 * 2**20, transcendentals=0),
        name="filter_step",
    )(
        previous.reshape(N, rows, X),
        current.reshape(N, rows, X),
        potential.reshape(rows, X),
        projectors.reshape(NPR, rows, X),
        couplings,
        pattern,
        counts,
        panels.reshape(SHARD, rows, X),
    )
    return rotated.reshape(N, C, C, X), coefs.T


def solution(mesh):
    in_specs = (
        P("band", "gy", "gz", None),
        P("band", "gy", "gz", None),
        P("gy", "gz", None),
        P(None, "gy", "gz", None),
        P(),
        P(),
        P(),
        P("band", "gy", "gz", None),
    )
    out_specs = (P("band", "gy", "gz", None), P(None, "band"))
    return jax.shard_map(
        per_device, mesh=mesh, in_specs=in_specs, out_specs=out_specs, check_vma=False
    )
```

```python
import jax
import jax.numpy as jnp
from jax import lax
from jax.experimental import pallas as pl
from jax.experimental.pallas import tpu as pltpu
from jax.sharding import PartitionSpec as P

STENCIL = (
    -5369.0 / 1800.0,
    12.0 / 7.0,
    -15.0 / 56.0,
    10.0 / 189.0,
    -1.0 / 112.0,
    2.0 / 1925.0,
    -1.0 / 16632.0,
)
CENTER = 1.0
HALF_WIDTH = 5.0
SCALE = 2.0 / HALF_WIDTH

N = 16
C = 8
X = 128
NPR = 64
SHARD = 32
NP = 256
NEAR = 192
CHUNK = 8
F32 = jnp.float32
BF16 = jnp.bfloat16
MESH = pl.DeviceIdType.MESH
ANY = pl.BlockSpec(memory_space=pl.ANY)
SMEM = pl.BlockSpec(memory_space=pltpu.SMEM)


def split(value):
    high = value.astype(BF16)
    return high, (value - high.astype(F32)).astype(BF16)


def same_layer(rows, columns):
    row = lax.broadcasted_iota(jnp.int32, (rows, columns), 0)
    column = lax.broadcasted_iota(jnp.int32, (rows, columns), 1)
    return (row & 7) == (column & 7)


def dot(left, right):
    return jnp.dot(left, right, preferred_element_type=F32)


def convert(source, target, first, count):
    @pl.loop(0, count // 16)
    def _(step):
        start = pl.multiple_of(first + step * 16, 8)
        row = pl.multiple_of(start * 8, 64)
        for y in range(C):
            rows = source[pl.ds(start, 16), y * 8 : y * 8 + 8, :].reshape(128, X)
            high, low = split(rows)
            target[pl.ds(row, 128), y * X : (y + 1) * X] = high
            target[pl.ds(row, 128), (C + y) * X : (C + y + 1) * X] = low


def transpose_block(source, target):
    for y in range(C):
        rows = source[:, y * 8 : y * 8 + 8, :].reshape(N * 8, X).T
        high, low = split(rows)
        target[y * X : (y + 1) * X, 0:128] = high
        target[y * X : (y + 1) * X, 128:256] = low


def contract(table, block, sums, first, count):
    @pl.loop(0, count // 32)
    def _(step):
        start = pl.multiple_of(first + step * 32, 32)
        rows = pl.ds(pl.multiple_of(start * 8, 256), 256)
        full = dot(table[rows, 0:1024], block[...]) + dot(table[rows, 1024:2048], block[...])
        both = full[:, 0:128] + full[:, 128:256]
        kept = jnp.where(same_layer(256, 128), both, 0.0)
        sums[pl.ds(start, 32), :] = kept.reshape(32, 8, 128).sum(axis=1)


def fold_layers(sums):
    band = lax.broadcasted_iota(jnp.int32, (N, 128), 0)
    column = lax.broadcasted_iota(jnp.int32, (N, 128), 1)
    ones = jnp.where(band == (column >> 3), 1.0, 0.0).astype(F32)
    return lax.dot_general(
        ones,
        sums,
        (((1,), (1,)), ((), ())),
        precision=lax.Precision.HIGHEST,
        preferred_element_type=F32,
    )


def pack(coefs):
    return jnp.concatenate([coefs[0:8], coefs[8:16]], axis=1)


def unpack(packed):
    return jnp.concatenate([packed[:, 0:64], packed[:, 64:128]], axis=0)


def spread(coefs, repeat, target, first):
    count = coefs.shape[1]
    columns = count * 8
    wide = jnp.broadcast_to(coefs[:, None, :], (N, 8, count)).reshape(N * 8, count)
    high, low = split(wide)
    both = jnp.concatenate([high, low], axis=0)
    for at in range(0, columns, 256):
        values = dot(both, repeat[0:count, at : at + 256])
        target[:, first + at : first + at + 256] = jnp.where(same_layer(256, 256), values, 0.0).astype(BF16)


def kernel(
    prev_hbm, cur_hbm, pot_hbm, proj_hbm, coup, pattern, counts, pan_hbm,
    out_hbm, coef_out,
    cur, turned, y_low, y_high, z_low, z_high, filt, prev, pot, proj, proj_split,
    gathered, pan_split, block, repeat, spread_ref, sums, small_a, small_b, near_a, near_b, far_a, far_b,
    load_sem, halo_send, halo_recv, right_send, left_recv, left_send, right_recv,
    sib_send, sib_recv, ahead_send, behind_recv, back_send, front_recv,
    sum_send, sum_recv, store_sem,
):
    gy, gz, band = lax.axis_index("gy"), lax.axis_index("gz"), lax.axis_index("band")
    z_hi, y = gy // 8, gy % 8
    z = z_hi * 4 + gz
    x, core = band // 2, band % 2

    def at_y(other):
        return {"gy": z_hi * 8 + other, "gz": gz, "band": band}

    def at_z(other):
        return {"gy": (other // 4) * 8 + y, "gz": other % 4, "band": band}

    def at_band(other):
        return {"gy": gy, "gz": gz, "band": other}

    up_y = {"gy": (gy + 1) % 16, "gz": gz, "band": band}
    down_y = {"gy": (gy + 15) % 16, "gz": gz, "band": band}
    up_z = {"gy": gy, "gz": (gz + 1) % 4, "band": band}
    down_z = {"gy": gy, "gz": (gz + 3) % 4, "band": band}
    right, left = ((x + 1) % 4) * 2 + core, ((x + 3) % 4) * 2 + core
    opposite, sibling = ((x + 2) % 4) * 2 + core, x * 2 + 1 - core

    own_at, right_at, left_at, opposite_at = 0, 2, 4, 6
    owners = [band, sibling]
    for chip in (right, left, opposite):
        owners += [chip, chip + 1 - 2 * core]
    load_pan = pltpu.make_async_copy(pan_hbm, gathered.at[pl.ds(0, SHARD)], load_sem.at[0])
    load_cur = pltpu.make_async_copy(cur_hbm, cur, load_sem.at[1])
    load_proj = pltpu.make_async_copy(proj_hbm, proj, load_sem.at[2])
    load_prev = pltpu.make_async_copy(prev_hbm, prev, load_sem.at[3])
    load_pot = pltpu.make_async_copy(pot_hbm, pot, load_sem.at[4])
    for load in (load_pan, load_cur, load_proj, load_prev, load_pot):
        load.start()

    barrier = pltpu.get_barrier_semaphore()
    partners = [at_y((y + r) % 8) for r in range(1, 8)]
    partners += [at_z((z + r) % 8) for r in range(1, 8)]
    partners += [up_y, down_y, up_z, down_z]
    partners += [at_band(right), at_band(left), at_band(sibling)]
    for partner in partners:
        pl.semaphore_signal(barrier, inc=1, device_id=partner, device_id_type=MESH)
    pl.semaphore_wait(barrier, len(partners))

    def remote(source, target, send, recv, device):
        return pltpu.make_async_remote_copy(
            src_ref=source, dst_ref=target, send_sem=send, recv_sem=recv,
            device_id=device, device_id_type=MESH,
        )

    def panel_copy(slot, there, k, send, recv, device):
        source = gathered.at[pl.ds(slot * SHARD + k * CHUNK, CHUNK)]
        target = gathered.at[pl.ds(there * SHARD + k * CHUNK, CHUNK)]
        return remote(source, target, send, recv, device)

    def to_right(slot, there, k, sems, recvs, at):
        return panel_copy(slot, there, k, sems.at[at], recvs.at[at], at_band(right))

    def to_left(slot, there, k, sems, recvs, at):
        return panel_copy(slot, there, k, sems.at[at], recvs.at[at], at_band(left))

    def to_sibling(slot, k):
        at = slot // 2 * 4 + k
        return panel_copy(slot, slot + 1, k, sib_send.at[at], sib_recv.at[at], at_band(sibling))

    load_pan.wait()
    started = []

    def pass_on(copy):
        copy.start()
        started.append(copy)

    for step in range(4):
        k = step
        pass_on(to_right(own_at, left_at, k, right_send, left_recv, k))
        k = (step + 2) % 4
        pass_on(to_left(own_at, right_at, k, left_send, right_recv, k))
    for k in range(4):
        pass_on(to_sibling(own_at, k))

    load_cur.wait()
    halo_y0 = remote(cur.at[:, pl.ds(16, 48)], y_low, halo_send.at[0], halo_recv.at[0], up_y)
    halo_y1 = remote(cur.at[:, pl.ds(0, 48)], y_high, halo_send.at[1], halo_recv.at[1], down_y)
    halo_y0.start()
    halo_y1.start()

    @pl.loop(0, N)
    def _(n):
        for layer in range(C):
            turned[n, layer * 8 : layer * 8 + 8, :] = cur[n, pl.ds(layer, 8, stride=8), :]

    halo_z0 = remote(turned.at[:, pl.ds(16, 48)], z_low, halo_send.at[2], halo_recv.at[2], up_z)
    halo_z1 = remote(turned.at[:, pl.ds(0, 48)], z_high, halo_send.at[3], halo_recv.at[3], down_z)
    halo_z0.start()
    halo_z1.start()

    transpose_block(cur, block)
    load_proj.wait()
    convert(proj, proj_split, 0, NPR)
    contract(proj_split, block, sums, 0, NPR)

    lane = lax.broadcasted_iota(jnp.int32, (N, NPR), 1)
    tile = gy * 4 + gz
    weight = jnp.zeros((N, NPR), F32)
    for b in range(8):
        reached = pattern[b, tile].astype(F32)
        live = ((lane >> 3) == b) & ((lane & 7) < counts[b])
        weight = jnp.where(live, reached, weight)
    coupling = jnp.zeros((N, NPR), F32)
    for j in range(NPR):
        coupling = jnp.where(lane == j, coup[j], coupling)

    def send_y(buffer, sems):
        copies = []
        for r in range(1, 8):
            copies.append(
                remote(buffer.at[y], buffer.at[y], sum_send.at[sems, r], sum_recv.at[sems, y], at_y((y + r) % 8))
            )
            copies[-1].start()
        return copies

    def send_z(buffer, sems):
        copies = []
        for r in range(1, 8):
            copies.append(
                remote(buffer.at[z], buffer.at[z], sum_send.at[sems, r], sum_recv.at[sems, z], at_z((z + r) % 8))
            )
            copies[-1].start()
        return copies

    def receive(buffer, sems, me):
        for r in range(1, 8):
            other = (me + r) % 8
            remote(buffer.at[other], buffer.at[other], sum_send.at[sems, r], sum_recv.at[sems, other], up_y).wait_recv()

    def total(buffer):
        value = buffer[0]
        for i in range(1, 8):
            value = value + buffer[i]
        return value

    small_a[y] = pack(fold_layers(sums[0:NPR, :]) * weight)
    sent = send_y(small_a, 0)

    load_prev.wait()
    load_pot.wait()

    @pl.loop(0, N)
    def _(n):
        value = cur[n]
        lap = 3.0 * STENCIL[0] * value
        for reach in range(1, 7):
            lap = lap + STENCIL[reach] * (pltpu.roll(value, reach, 1) + pltpu.roll(value, X - reach, 1))
        filt[n] = SCALE * (-0.5 * lap + pot[...] * value - CENTER * value) - prev[n]

    receive(small_a, 0, y)
    small_b[z] = total(small_a)
    sent += send_z(small_b, 1)

    @pl.loop(0, 6)
    def _(step):
        at = pl.multiple_of(step * 256, 256)
        row = lax.broadcasted_iota(jnp.int32, (NEAR, 256), 0)
        column = lax.broadcasted_iota(jnp.int32, (NEAR, 256), 1) + at
        repeat[:, pl.ds(at, 256)] = jnp.where(row == (column >> 3), 1.0, 0.0).astype(BF16)

    convert(gathered, pan_split, 0, SHARD)

    for step in range(4):
        k = step
        to_right(own_at, left_at, k, right_send, left_recv, k).wait_recv()
        if k < 2:
            pass_on(to_right(left_at, opposite_at, k, ahead_send, behind_recv, k))
        pass_on(to_sibling(left_at, k))
        k = (step + 2) % 4
        to_left(own_at, right_at, k, left_send, right_recv, k).wait_recv()
        if k >= 2:
            pass_on(to_left(right_at, opposite_at, k, back_send, front_recv, k - 2))
        pass_on(to_sibling(right_at, k))

    def take(slot):
        for k in range(4):
            to_sibling(slot, k).wait_recv()

    take(own_at)
    convert(gathered, pan_split, SHARD, SHARD)
    convert(gathered, pan_split, right_at * SHARD, SHARD)
    convert(gathered, pan_split, left_at * SHARD, SHARD)

    receive(small_b, 1, z)
    spread(unpack(total(small_b)) * (coupling * weight), repeat, spread_ref, 0)
    for part in range(4):
        at = part * 256
        value = dot(spread_ref[:, 0:512], proj_split[:, at : at + 256])
        value = value[0:128] + value[128:256] + dot(spread_ref[0:128, 0:512], proj_split[:, 1024 + at : 1280 + at])
        for half in range(2):
            rows = pl.ds((part * 2 + half) * 8, 8)
            filt[:, rows, :] += SCALE * value[:, half * X : (half + 1) * X].reshape(N, 8, X)

    take(right_at)
    convert(gathered, pan_split, (right_at + 1) * SHARD, SHARD)
    take(left_at)
    convert(gathered, pan_split, (left_at + 1) * SHARD, SHARD)

    halo_y0.wait_recv()
    halo_y1.wait_recv()

    def stencil(rows):
        result = []
        for at in range(C):
            value = None
            for reach in range(1, 7):
                pair = STENCIL[reach] * (rows[6 + at + reach] + rows[6 + at - reach])
                value = pair if value is None else value + pair
            result.append(-0.5 * SCALE * value)
        return result

    def lines(ref, n, count):
        return [ref[n, i * 8 : i * 8 + 8, :] for i in range(count)]

    @pl.loop(0, N)
    def _(n):
        parts = stencil(lines(y_low, n, 6) + lines(cur, n, 8) + lines(y_high, n, 6))
        for at in range(C):
            filt[n, at * 8 : at * 8 + 8, :] += parts[at]

    for k in (0, 1):
        to_right(left_at, opposite_at, k, ahead_send, behind_recv, k).wait_recv()
        pass_on(to_sibling(opposite_at, k))
        to_left(right_at, opposite_at, k + 2, back_send, front_recv, k).wait_recv()
        pass_on(to_sibling(opposite_at, k + 2))

    halo_z0.wait_recv()
    halo_z1.wait_recv()

    @pl.loop(0, N)
    def _(n):
        parts = stencil(lines(z_low, n, 6) + lines(turned, n, 8) + lines(z_high, n, 6))
        for at in range(C):
            filt[n, pl.ds(at, 8, stride=8), :] += parts[at]

    transpose_block(filt, block)

    contract(pan_split, block, sums, 0, NEAR)
    near = fold_layers(sums[0:NEAR, :])
    near_a[y, 0:16, :] = near[:, 0:128]
    near_a[y, 16:24, :] = pack(near[:, 128:NEAR])
    sent += send_y(near_a, 2)
    convert(gathered, pan_split, opposite_at * SHARD, SHARD)
    take(opposite_at)
    convert(gathered, pan_split, (opposite_at + 1) * SHARD, SHARD)
    contract(pan_split, block, sums, NEAR, NP - NEAR)
    far_a[y] = pack(fold_layers(sums[NEAR:NP, :]))
    sent += send_y(far_a, 3)
    receive(near_a, 2, y)
    near_b[z] = total(near_a)
    sent += send_z(near_b, 4)
    receive(far_a, 3, y)
    far_b[z] = total(far_a)
    sent += send_z(far_b, 5)

    def take_away(first, count, part):
        at = part * 256
        table = pl.ds(first * 8, count * 8)
        value = dot(spread_ref[:, table], pan_split[table, at : at + 256])
        value = value[0:128] + value[128:256] + dot(spread_ref[0:128, table], pan_split[table, 1024 + at : 1280 + at])
        for half in range(2):
            rows = pl.ds((part * 2 + half) * 8, 8)
            filt[:, rows, :] -= value[:, half * X : (half + 1) * X].reshape(N, 8, X)

    def write_coefs(coefs, slot):
        values = coefs.T
        for i in range(coefs.shape[1] // SHARD):
            rows = pl.ds(pl.multiple_of(owners[slot + i] * SHARD, SHARD), SHARD)
            coef_out[rows, :] = values[i * SHARD : (i + 1) * SHARD, :]

    receive(near_b, 4, z)
    packed = total(near_b)
    near = jnp.concatenate([packed[0:16], unpack(packed[16:24])], axis=1)
    spread(near, repeat, spread_ref, 0)
    for part in range(4):
        take_away(0, NEAR, part)
    write_coefs(near, 0)
    receive(far_b, 5, z)
    far = unpack(total(far_b))
    spread(far, repeat, spread_ref, NEAR * 8)
    stores = []
    for part in range(4):
        take_away(NEAR, NP - NEAR, part)
        rows = pl.ds(part * 16, 16)
        stores.append(pltpu.make_async_copy(filt.at[:, rows], out_hbm.at[:, rows], store_sem.at[part]))
        stores[-1].start()
    write_coefs(far, opposite_at)

    for copy in started + sent + [halo_y0, halo_y1, halo_z0, halo_z1]:
        copy.wait_send()
    for copy in stores:
        copy.wait()


def per_device(previous, current, potential, projectors, couplings, pattern, counts, panels):
    rows = C * C
    vmem = pltpu.VMEM
    dma = pltpu.SemaphoreType.DMA
    rotated, coefs = pl.pallas_call(
        kernel,
        out_shape=(
            jax.ShapeDtypeStruct((N, rows, X), F32),
            jax.ShapeDtypeStruct((NP, N), F32),
        ),
        in_specs=[ANY, ANY, ANY, ANY, SMEM, SMEM, SMEM, ANY],
        out_specs=(ANY, pl.BlockSpec(memory_space=pltpu.VMEM)),
        scratch_shapes=[
            vmem((N, rows, X), F32),
            vmem((N, rows, X), F32),
            vmem((N, 48, X), F32),
            vmem((N, 48, X), F32),
            vmem((N, 48, X), F32),
            vmem((N, 48, X), F32),
            vmem((N, rows, X), F32),
            vmem((N, rows, X), F32),
            vmem((rows, X), F32),
            vmem((NPR, rows, X), F32),
            vmem((NPR * 8, 2048), BF16),
            vmem((NP, rows, X), F32),
            vmem((NP * 8, 2048), BF16),
            vmem((1024, 256), BF16),
            vmem((NEAR, 1536), BF16),
            vmem((256, 2048), BF16),
            vmem((NP, 128), F32),
            vmem((8, 8, 128), F32),
            vmem((8, 8, 128), F32),
            vmem((8, 24, 128), F32),
            vmem((8, 24, 128), F32),
            vmem((8, 8, 128), F32),
            vmem((8, 8, 128), F32),
            dma((5,)),
            dma((4,)),
            dma((4,)),
            dma((4,)),
            dma((4,)),
            dma((4,)),
            dma((4,)),
            dma((16,)),
            dma((16,)),
            dma((2,)),
            dma((2,)),
            dma((2,)),
            dma((2,)),
            dma((6, 8)),
            dma((6, 8)),
            dma((4,)),
        ],
        compiler_params=pltpu.CompilerParams(
            collective_id=0, has_side_effects=True, vmem_limit_bytes=56 * 1024 * 1024
        ),
        cost_estimate=pl.CostEstimate(flops=10**9, bytes_accessed=5 * 2**20, transcendentals=0),
        name="filter_step",
    )(
        previous.reshape(N, rows, X),
        current.reshape(N, rows, X),
        potential.reshape(rows, X),
        projectors.reshape(NPR, rows, X),
        couplings,
        pattern,
        counts,
        panels.reshape(SHARD, rows, X),
    )
    return rotated.reshape(N, C, C, X), coefs


def solution(mesh):
    in_specs = (
        P("band", "gy", "gz", None),
        P("band", "gy", "gz", None),
        P("gy", "gz", None),
        P(None, "gy", "gz", None),
        P(),
        P(),
        P(),
        P("band", "gy", "gz", None),
    )
    out_specs = (P("band", "gy", "gz", None), P(None, "band"))
    return jax.shard_map(
        per_device, mesh=mesh, in_specs=in_specs, out_specs=out_specs, check_vma=False
    )
```

```python
import jax
import jax.numpy as jnp
from jax import lax
from jax.experimental import pallas as pl
from jax.experimental.pallas import tpu as pltpu
from jax.sharding import PartitionSpec as P

STENCIL = (
    -5369.0 / 1800.0,
    12.0 / 7.0,
    -15.0 / 56.0,
    10.0 / 189.0,
    -1.0 / 112.0,
    2.0 / 1925.0,
    -1.0 / 16632.0,
)
CENTER = 1.0
HALF_WIDTH = 5.0
SCALE = 2.0 / HALF_WIDTH

N = 16
C = 8
X = 128
NPR = 64
SHARD = 32
NP = 256
NEAR = 192
CHUNK = 8
DIRECT = 8
F32 = jnp.float32
BF16 = jnp.bfloat16
MESH = pl.DeviceIdType.MESH
ANY = pl.BlockSpec(memory_space=pl.ANY)
SMEM = pl.BlockSpec(memory_space=pltpu.SMEM)


def split(value):
    high = value.astype(BF16)
    return high, (value - high.astype(F32)).astype(BF16)


def same_layer(rows, columns):
    row = lax.broadcasted_iota(jnp.int32, (rows, columns), 0)
    column = lax.broadcasted_iota(jnp.int32, (rows, columns), 1)
    return (row & 7) == (column & 7)


def dot(left, right):
    return jnp.dot(left, right, preferred_element_type=F32)


def convert(source, target, first, count):
    @pl.loop(0, count // 16)
    def _(step):
        start = pl.multiple_of(first + step * 16, 8)
        row = pl.multiple_of(start * 8, 64)
        for y in range(C):
            rows = source[pl.ds(start, 16), y * 8 : y * 8 + 8, :].reshape(128, X)
            high, low = split(rows)
            target[pl.ds(row, 128), y * X : (y + 1) * X] = high
            target[pl.ds(row, 128), (C + y) * X : (C + y + 1) * X] = low


def transpose_block(source, target):
    for y in range(C):
        rows = source[:, y * 8 : y * 8 + 8, :].reshape(N * 8, X).T
        high, low = split(rows)
        target[y * X : (y + 1) * X, 0:128] = high
        target[y * X : (y + 1) * X, 128:256] = low


def contract(table, block, sums, first, count):
    @pl.loop(0, count // 32)
    def _(step):
        start = pl.multiple_of(first + step * 32, 32)
        rows = pl.ds(pl.multiple_of(start * 8, 256), 256)
        full = dot(table[rows, 0:1024], block[...]) + dot(table[rows, 1024:2048], block[...])
        both = full[:, 0:128] + full[:, 128:256]
        kept = jnp.where(same_layer(256, 128), both, 0.0)
        sums[pl.ds(start, 32), :] = kept.reshape(32, 8, 128).sum(axis=1)


def fold_layers(sums):
    band = lax.broadcasted_iota(jnp.int32, (N, 128), 0)
    column = lax.broadcasted_iota(jnp.int32, (N, 128), 1)
    ones = jnp.where(band == (column >> 3), 1.0, 0.0).astype(F32)
    return lax.dot_general(
        ones,
        sums,
        (((1,), (1,)), ((), ())),
        precision=lax.Precision.HIGHEST,
        preferred_element_type=F32,
    )


def pack(coefs):
    return jnp.concatenate([coefs[0:8], coefs[8:16]], axis=1)


def unpack(packed):
    return jnp.concatenate([packed[:, 0:64], packed[:, 64:128]], axis=0)


def spread(coefs, repeat, target, first):
    count = coefs.shape[1]
    columns = count * 8
    wide = jnp.broadcast_to(coefs[:, None, :], (N, 8, count)).reshape(N * 8, count)
    high, low = split(wide)
    both = jnp.concatenate([high, low], axis=0)
    for at in range(0, columns, 256):
        values = dot(both, repeat[0:count, at : at + 256])
        target[:, first + at : first + at + 256] = jnp.where(same_layer(256, 256), values, 0.0).astype(BF16)


def kernel(
    prev_hbm, cur_hbm, pot_hbm, proj_hbm, coup, pattern, counts, pan_hbm,
    out_hbm, coef_out,
    cur, turned, y_low, y_high, z_low, z_high, filt, prev, pot, proj, proj_split,
    gathered, pan_split, block, repeat, spread_ref, sums, small_a, small_b, near_a, near_b, far_a, far_b, held,
    load_sem, halo_send, halo_recv, rest_send, rest_recv, right_send, left_recv, left_send, right_recv,
    sib_send, sib_recv, ahead_send, behind_recv, back_send, front_recv,
    sum_send, sum_recv, store_sem,
):
    gy, gz, band = lax.axis_index("gy"), lax.axis_index("gz"), lax.axis_index("band")
    z_hi, y = gy // 8, gy % 8
    z = z_hi * 4 + gz
    x, core = band // 2, band % 2

    def at_y(other):
        return {"gy": z_hi * 8 + other, "gz": gz, "band": band}

    def at_z(other):
        return {"gy": (other // 4) * 8 + y, "gz": other % 4, "band": band}

    def at_band(other):
        return {"gy": gy, "gz": gz, "band": other}

    up_y = {"gy": (gy + 1) % 16, "gz": gz, "band": band}
    down_y = {"gy": (gy + 15) % 16, "gz": gz, "band": band}
    up_z = {"gy": gy, "gz": (gz + 1) % 4, "band": band}
    down_z = {"gy": gy, "gz": (gz + 3) % 4, "band": band}
    right, left = ((x + 1) % 4) * 2 + core, ((x + 3) % 4) * 2 + core
    opposite, sibling = ((x + 2) % 4) * 2 + core, x * 2 + 1 - core

    own_at, right_at, left_at, opposite_at = 0, 2, 4, 6
    owners = [band, sibling]
    for chip in (right, left, opposite):
        owners += [chip, chip + 1 - 2 * core]
    load_pan = pltpu.make_async_copy(pan_hbm, gathered.at[pl.ds(0, SHARD)], load_sem.at[0])
    load_cur = pltpu.make_async_copy(cur_hbm, cur, load_sem.at[1])
    load_proj = pltpu.make_async_copy(proj_hbm, proj, load_sem.at[2])
    load_prev = pltpu.make_async_copy(prev_hbm, prev, load_sem.at[3])
    load_pot = pltpu.make_async_copy(pot_hbm, pot, load_sem.at[4])
    for load in (load_pan, load_cur, load_proj, load_prev, load_pot):
        load.start()

    barrier = pltpu.get_barrier_semaphore()
    partners = [at_y((y + r) % 8) for r in range(1, 8)]
    partners += [at_z((z + r) % 8) for r in range(1, 8)]
    partners += [up_y, down_y, up_z, down_z]
    partners += [at_band(right), at_band(left), at_band(sibling)]
    over = (1 - z_hi) * 8
    after_wrap = {"gy": over + (8 - y) % 8, "gz": gz, "band": band}
    before_wrap = {"gy": over + (14 - y) % 8, "gz": gz, "band": band}
    partners += [after_wrap, before_wrap]
    for partner in partners:
        pl.semaphore_signal(barrier, inc=1, device_id=partner, device_id_type=MESH)
    pl.semaphore_wait(barrier, len(partners))

    def remote(source, target, send, recv, device):
        return pltpu.make_async_remote_copy(
            src_ref=source, dst_ref=target, send_sem=send, recv_sem=recv,
            device_id=device, device_id_type=MESH,
        )

    def panel_copy(slot, there, k, send, recv, device):
        source = gathered.at[pl.ds(slot * SHARD + k * CHUNK, CHUNK)]
        target = gathered.at[pl.ds(there * SHARD + k * CHUNK, CHUNK)]
        return remote(source, target, send, recv, device)

    def to_right(slot, there, k, sems, recvs, at):
        return panel_copy(slot, there, k, sems.at[at], recvs.at[at], at_band(right))

    def to_left(slot, there, k, sems, recvs, at):
        return panel_copy(slot, there, k, sems.at[at], recvs.at[at], at_band(left))

    def to_sibling(slot, k):
        at = slot // 2 * 4 + k
        return panel_copy(slot, slot + 1, k, sib_send.at[at], sib_recv.at[at], at_band(sibling))

    load_pan.wait()
    started = []

    def pass_on(copy):
        copy.start()
        started.append(copy)

    for step in range(4):
        k = step
        pass_on(to_right(own_at, left_at, k, right_send, left_recv, k))
        k = (step + 2) % 4
        pass_on(to_left(own_at, right_at, k, left_send, right_recv, k))
    for k in range(4):
        pass_on(to_sibling(own_at, k))

    load_cur.wait()
    first, rest = pl.ds(0, DIRECT), pl.ds(DIRECT, N - DIRECT)
    upper, lower = pl.ds(16, 48), pl.ds(0, 48)
    halo_y0 = remote(cur.at[first, upper], y_low.at[first], halo_send.at[0], halo_recv.at[0], up_y)
    halo_y1 = remote(cur.at[first, lower], y_high.at[first], halo_send.at[1], halo_recv.at[1], down_y)
    rest_y0 = remote(cur.at[rest, upper], y_low.at[rest], rest_send.at[0], rest_recv.at[0], up_y)
    rest_y1 = remote(cur.at[rest, lower], y_high.at[rest], rest_send.at[1], rest_recv.at[1], down_y)
    around_y0 = remote(cur.at[rest, upper], held, rest_send.at[0], rest_recv.at[2], after_wrap)
    around_y1 = remote(cur.at[rest, lower], held, rest_send.at[1], rest_recv.at[2], before_wrap)
    onward_y0 = remote(held, y_low.at[rest], rest_send.at[2], rest_recv.at[0], down_y)
    onward_y1 = remote(held, y_high.at[rest], rest_send.at[2], rest_recv.at[1], up_y)

    def under(condition, action):
        @pl.when(condition)
        def _():
            action()

    under(y == 7, around_y0.start)
    under(y == 0, around_y1.start)
    under(y != 7, rest_y0.start)
    under(y != 0, rest_y1.start)
    halo_y0.start()
    halo_y1.start()

    @pl.loop(0, N)
    def _(n):
        for layer in range(C):
            turned[n, layer * 8 : layer * 8 + 8, :] = cur[n, pl.ds(layer, 8, stride=8), :]

    halo_z0 = remote(turned.at[:, pl.ds(16, 48)], z_low, halo_send.at[2], halo_recv.at[2], up_z)
    halo_z1 = remote(turned.at[:, pl.ds(0, 48)], z_high, halo_send.at[3], halo_recv.at[3], down_z)
    halo_z0.start()
    halo_z1.start()

    transpose_block(cur, block)
    load_proj.wait()
    convert(proj, proj_split, 0, NPR)
    contract(proj_split, block, sums, 0, NPR)

    lane = lax.broadcasted_iota(jnp.int32, (N, NPR), 1)
    tile = gy * 4 + gz
    weight = jnp.zeros((N, NPR), F32)
    for b in range(8):
        reached = pattern[b, tile].astype(F32)
        live = ((lane >> 3) == b) & ((lane & 7) < counts[b])
        weight = jnp.where(live, reached, weight)
    coupling = jnp.zeros((N, NPR), F32)
    for j in range(NPR):
        coupling = jnp.where(lane == j, coup[j], coupling)

    def send_y(buffer, sems):
        copies = []
        for r in range(1, 8):
            copies.append(
                remote(buffer.at[y], buffer.at[y], sum_send.at[sems, r], sum_recv.at[sems, y], at_y((y + r) % 8))
            )
            copies[-1].start()
        return copies

    def send_z(buffer, sems):
        copies = []
        for r in range(1, 8):
            copies.append(
                remote(buffer.at[z], buffer.at[z], sum_send.at[sems, r], sum_recv.at[sems, z], at_z((z + r) % 8))
            )
            copies[-1].start()
        return copies

    def receive(buffer, sems, me):
        for r in range(1, 8):
            other = (me + r) % 8
            remote(buffer.at[other], buffer.at[other], sum_send.at[sems, r], sum_recv.at[sems, other], up_y).wait_recv()

    def total(buffer):
        value = buffer[0]
        for i in range(1, 8):
            value = value + buffer[i]
        return value

    small_a[y] = pack(fold_layers(sums[0:NPR, :]) * weight)
    sent = send_y(small_a, 0)

    load_prev.wait()
    load_pot.wait()

    @pl.loop(0, N)
    def _(n):
        value = cur[n]
        lap = 3.0 * STENCIL[0] * value
        for reach in range(1, 7):
            lap = lap + STENCIL[reach] * (pltpu.roll(value, reach, 1) + pltpu.roll(value, X - reach, 1))
        filt[n] = SCALE * (-0.5 * lap + pot[...] * value - CENTER * value) - prev[n]

    receive(small_a, 0, y)
    small_b[z] = total(small_a)
    sent += send_z(small_b, 1)

    @pl.loop(0, 6)
    def _(step):
        at = pl.multiple_of(step * 256, 256)
        row = lax.broadcasted_iota(jnp.int32, (NEAR, 256), 0)
        column = lax.broadcasted_iota(jnp.int32, (NEAR, 256), 1) + at
        repeat[:, pl.ds(at, 256)] = jnp.where(row == (column >> 3), 1.0, 0.0).astype(BF16)

    convert(gathered, pan_split, 0, SHARD)

    for step in range(4):
        k = step
        to_right(own_at, left_at, k, right_send, left_recv, k).wait_recv()
        if k < 2:
            pass_on(to_right(left_at, opposite_at, k, ahead_send, behind_recv, k))
        pass_on(to_sibling(left_at, k))
        k = (step + 2) % 4
        to_left(own_at, right_at, k, left_send, right_recv, k).wait_recv()
        if k >= 2:
            pass_on(to_left(right_at, opposite_at, k, back_send, front_recv, k - 2))
        pass_on(to_sibling(right_at, k))

    @pl.when(y == 1)
    def _():
        around_y0.wait_recv()
        onward_y0.start()

    @pl.when(y == 6)
    def _():
        around_y1.wait_recv()
        onward_y1.start()

    def take(slot):
        for k in range(4):
            to_sibling(slot, k).wait_recv()

    take(own_at)
    convert(gathered, pan_split, SHARD, SHARD)
    convert(gathered, pan_split, right_at * SHARD, SHARD)
    convert(gathered, pan_split, left_at * SHARD, SHARD)

    receive(small_b, 1, z)
    spread(unpack(total(small_b)) * (coupling * weight), repeat, spread_ref, 0)
    for part in range(4):
        at = part * 256
        value = dot(spread_ref[:, 0:512], proj_split[:, at : at + 256])
        value = value[0:128] + value[128:256] + dot(spread_ref[0:128, 0:512], proj_split[:, 1024 + at : 1280 + at])
        for half in range(2):
            rows = pl.ds((part * 2 + half) * 8, 8)
            filt[:, rows, :] += SCALE * value[:, half * X : (half + 1) * X].reshape(N, 8, X)

    take(right_at)
    convert(gathered, pan_split, (right_at + 1) * SHARD, SHARD)
    take(left_at)
    convert(gathered, pan_split, (left_at + 1) * SHARD, SHARD)

    for copy in (halo_y0, halo_y1, rest_y0, rest_y1):
        copy.wait_recv()

    def stencil(rows):
        result = []
        for at in range(C):
            value = None
            for reach in range(1, 7):
                pair = STENCIL[reach] * (rows[6 + at + reach] + rows[6 + at - reach])
                value = pair if value is None else value + pair
            result.append(-0.5 * SCALE * value)
        return result

    def lines(ref, n, count):
        return [ref[n, i * 8 : i * 8 + 8, :] for i in range(count)]

    @pl.loop(0, N)
    def _(n):
        parts = stencil(lines(y_low, n, 6) + lines(cur, n, 8) + lines(y_high, n, 6))
        for at in range(C):
            filt[n, at * 8 : at * 8 + 8, :] += parts[at]

    halo_z0.wait_recv()
    halo_z1.wait_recv()

    @pl.loop(0, N)
    def _(n):
        parts = stencil(lines(z_low, n, 6) + lines(turned, n, 8) + lines(z_high, n, 6))
        for at in range(C):
            filt[n, pl.ds(at, 8, stride=8), :] += parts[at]

    transpose_block(filt, block)

    contract(pan_split, block, sums, 0, NEAR)
    near = fold_layers(sums[0:NEAR, :])
    near_a[y, 0:16, :] = near[:, 0:128]
    near_a[y, 16:24, :] = pack(near[:, 128:NEAR])
    sent += send_y(near_a, 2)
    for k in (0, 1):
        to_right(left_at, opposite_at, k, ahead_send, behind_recv, k).wait_recv()
        pass_on(to_sibling(opposite_at, k))
        to_left(right_at, opposite_at, k + 2, back_send, front_recv, k).wait_recv()
        pass_on(to_sibling(opposite_at, k + 2))
    convert(gathered, pan_split, opposite_at * SHARD, SHARD)
    contract(pan_split, block, sums, NEAR, SHARD)
    take(opposite_at)
    convert(gathered, pan_split, (opposite_at + 1) * SHARD, SHARD)
    contract(pan_split, block, sums, NEAR + SHARD, SHARD)
    far_a[y] = pack(fold_layers(sums[NEAR:NP, :]))
    sent += send_y(far_a, 3)
    receive(near_a, 2, y)
    near_b[z] = total(near_a)
    sent += send_z(near_b, 4)
    receive(far_a, 3, y)
    far_b[z] = total(far_a)
    sent += send_z(far_b, 5)

    def take_away(first, count, part):
        at = part * 256
        table = pl.ds(first * 8, count * 8)
        value = dot(spread_ref[:, table], pan_split[table, at : at + 256])
        value = value[0:128] + value[128:256] + dot(spread_ref[0:128, table], pan_split[table, 1024 + at : 1280 + at])
        for half in range(2):
            rows = pl.ds((part * 2 + half) * 8, 8)
            filt[:, rows, :] -= value[:, half * X : (half + 1) * X].reshape(N, 8, X)

    def write_coefs(coefs, slot):
        values = coefs.T
        for i in range(coefs.shape[1] // SHARD):
            rows = pl.ds(pl.multiple_of(owners[slot + i] * SHARD, SHARD), SHARD)
            coef_out[rows, :] = values[i * SHARD : (i + 1) * SHARD, :]

    receive(near_b, 4, z)
    packed = total(near_b)
    near = jnp.concatenate([packed[0:16], unpack(packed[16:24])], axis=1)
    spread(near, repeat, spread_ref, 0)
    for part in range(4):
        take_away(0, NEAR, part)
    write_coefs(near, 0)
    receive(far_b, 5, z)
    far = unpack(total(far_b))
    spread(far, repeat, spread_ref, NEAR * 8)
    stores = []
    for part in range(4):
        take_away(NEAR, NP - NEAR, part)
        rows = pl.ds(part * 16, 16)
        stores.append(pltpu.make_async_copy(filt.at[:, rows], out_hbm.at[:, rows], store_sem.at[part]))
        stores[-1].start()
    write_coefs(far, opposite_at)

    for copy in started + sent + [halo_y0, halo_y1, rest_y0, rest_y1, halo_z0, halo_z1]:
        copy.wait_send()
    under((y == 1) | (y == 6), onward_y0.wait_send)
    for copy in stores:
        copy.wait()


def per_device(previous, current, potential, projectors, couplings, pattern, counts, panels):
    rows = C * C
    vmem = pltpu.VMEM
    dma = pltpu.SemaphoreType.DMA
    rotated, coefs = pl.pallas_call(
        kernel,
        out_shape=(
            jax.ShapeDtypeStruct((N, rows, X), F32),
            jax.ShapeDtypeStruct((NP, N), F32),
        ),
        in_specs=[ANY, ANY, ANY, ANY, SMEM, SMEM, SMEM, ANY],
        out_specs=(ANY, pl.BlockSpec(memory_space=pltpu.VMEM)),
        scratch_shapes=[
            vmem((N, rows, X), F32),
            vmem((N, rows, X), F32),
            vmem((N, 48, X), F32),
            vmem((N, 48, X), F32),
            vmem((N, 48, X), F32),
            vmem((N, 48, X), F32),
            vmem((N, rows, X), F32),
            vmem((N, rows, X), F32),
            vmem((rows, X), F32),
            vmem((NPR, rows, X), F32),
            vmem((NPR * 8, 2048), BF16),
            vmem((NP, rows, X), F32),
            vmem((NP * 8, 2048), BF16),
            vmem((1024, 256), BF16),
            vmem((NEAR, 1536), BF16),
            vmem((256, 2048), BF16),
            vmem((NP, 128), F32),
            vmem((8, 8, 128), F32),
            vmem((8, 8, 128), F32),
            vmem((8, 24, 128), F32),
            vmem((8, 24, 128), F32),
            vmem((8, 8, 128), F32),
            vmem((8, 8, 128), F32),
            vmem((N - DIRECT, 48, X), F32),
            dma((5,)),
            dma((4,)),
            dma((4,)),
            dma((3,)),
            dma((3,)),
            dma((4,)),
            dma((4,)),
            dma((4,)),
            dma((4,)),
            dma((16,)),
            dma((16,)),
            dma((2,)),
            dma((2,)),
            dma((2,)),
            dma((2,)),
            dma((6, 8)),
            dma((6, 8)),
            dma((4,)),
        ],
        compiler_params=pltpu.CompilerParams(
            collective_id=0, has_side_effects=True, vmem_limit_bytes=56 * 1024 * 1024
        ),
        cost_estimate=pl.CostEstimate(flops=10**9, bytes_accessed=5 * 2**20, transcendentals=0),
        name="filter_step",
    )(
        previous.reshape(N, rows, X),
        current.reshape(N, rows, X),
        potential.reshape(rows, X),
        projectors.reshape(NPR, rows, X),
        couplings,
        pattern,
        counts,
        panels.reshape(SHARD, rows, X),
    )
    return rotated.reshape(N, C, C, X), coefs


def solution(mesh):
    in_specs = (
        P("band", "gy", "gz", None),
        P("band", "gy", "gz", None),
        P("gy", "gz", None),
        P(None, "gy", "gz", None),
        P(),
        P(),
        P(),
        P("band", "gy", "gz", None),
    )
    out_specs = (P("band", "gy", "gz", None), P(None, "band"))
    return jax.shard_map(
        per_device, mesh=mesh, in_specs=in_specs, out_specs=out_specs, check_vma=False
    )
```

```python
import jax
import jax.numpy as jnp
from jax import lax
from jax.experimental import pallas as pl
from jax.experimental.pallas import tpu as pltpu
from jax.sharding import PartitionSpec as P

STENCIL = (
    -5369.0 / 1800.0,
    12.0 / 7.0,
    -15.0 / 56.0,
    10.0 / 189.0,
    -1.0 / 112.0,
    2.0 / 1925.0,
    -1.0 / 16632.0,
)
CENTER = 1.0
HALF_WIDTH = 5.0
SCALE = 2.0 / HALF_WIDTH

N = 16
C = 8
X = 128
NPR = 64
SHARD = 32
NP = 256
NEAR = 192
CHUNK = 8
PIECE = 4
DIRECT = 8
F32 = jnp.float32
BF16 = jnp.bfloat16
MESH = pl.DeviceIdType.MESH
ANY = pl.BlockSpec(memory_space=pl.ANY)
SMEM = pl.BlockSpec(memory_space=pltpu.SMEM)


def split(value):
    high = value.astype(BF16)
    return high, (value - high.astype(F32)).astype(BF16)


def same_layer(rows, columns):
    row = lax.broadcasted_iota(jnp.int32, (rows, columns), 0)
    column = lax.broadcasted_iota(jnp.int32, (rows, columns), 1)
    return (row & 7) == (column & 7)


def dot(left, right):
    return jnp.dot(left, right, preferred_element_type=F32)


def convert(source, target, first, count):
    @pl.loop(0, count // 16)
    def _(step):
        start = pl.multiple_of(first + step * 16, 8)
        row = pl.multiple_of(start * 8, 64)
        for y in range(C):
            rows = source[pl.ds(start, 16), y * 8 : y * 8 + 8, :].reshape(128, X)
            high, low = split(rows)
            target[pl.ds(row, 128), y * X : (y + 1) * X] = high
            target[pl.ds(row, 128), (C + y) * X : (C + y + 1) * X] = low


def transpose_block(source, target):
    for y in range(C):
        rows = source[:, y * 8 : y * 8 + 8, :].reshape(N * 8, X).T
        high, low = split(rows)
        target[y * X : (y + 1) * X, 0:128] = high
        target[y * X : (y + 1) * X, 128:256] = low


def contract(table, block, sums, first, count):
    @pl.loop(0, count // 32)
    def _(step):
        start = pl.multiple_of(first + step * 32, 32)
        rows = pl.ds(pl.multiple_of(start * 8, 256), 256)
        full = dot(table[rows, 0:1024], block[...]) + dot(table[rows, 1024:2048], block[...])
        both = full[:, 0:128] + full[:, 128:256]
        kept = jnp.where(same_layer(256, 128), both, 0.0)
        sums[pl.ds(start, 32), :] = kept.reshape(32, 8, 128).sum(axis=1)


def fold_layers(sums):
    band = lax.broadcasted_iota(jnp.int32, (N, 128), 0)
    column = lax.broadcasted_iota(jnp.int32, (N, 128), 1)
    ones = jnp.where(band == (column >> 3), 1.0, 0.0).astype(F32)
    return lax.dot_general(
        ones,
        sums,
        (((1,), (1,)), ((), ())),
        precision=lax.Precision.HIGHEST,
        preferred_element_type=F32,
    )


def pack(coefs):
    return jnp.concatenate([coefs[0:8], coefs[8:16]], axis=1)


def unpack(packed):
    return jnp.concatenate([packed[:, 0:64], packed[:, 64:128]], axis=0)


def spread(coefs, repeat, target, first):
    count = coefs.shape[1]
    columns = count * 8
    wide = jnp.broadcast_to(coefs[:, None, :], (N, 8, count)).reshape(N * 8, count)
    high, low = split(wide)
    both = jnp.concatenate([high, low], axis=0)
    for at in range(0, columns, 256):
        values = dot(both, repeat[0:count, at : at + 256])
        target[:, first + at : first + at + 256] = jnp.where(same_layer(256, 256), values, 0.0).astype(BF16)


def kernel(
    prev_hbm, cur_hbm, pot_hbm, proj_hbm, coup, pattern, counts, pan_hbm,
    out_hbm, coef_out,
    cur, turned, y_low, y_high, z_low, z_high, filt, prev, pot, proj, proj_split,
    gathered, pan_split, block, repeat, spread_ref, sums, small_a, small_b, near_a, near_b, far_a, far_b, held, coef_rows,
    load_sem, halo_send, halo_recv, rest_send, rest_recv, right_send, left_recv, left_send, right_recv,
    sib_send, sib_recv, ahead_send, behind_recv, back_send, front_recv,
    sum_send, sum_recv, store_sem,
):
    gy, gz, band = lax.axis_index("gy"), lax.axis_index("gz"), lax.axis_index("band")
    z_hi, y = gy // 8, gy % 8
    z = z_hi * 4 + gz
    x, core = band // 2, band % 2

    def at_y(other):
        return {"gy": z_hi * 8 + other, "gz": gz, "band": band}

    def at_z(other):
        return {"gy": (other // 4) * 8 + y, "gz": other % 4, "band": band}

    def at_band(other):
        return {"gy": gy, "gz": gz, "band": other}

    up_y = {"gy": (gy + 1) % 16, "gz": gz, "band": band}
    down_y = {"gy": (gy + 15) % 16, "gz": gz, "band": band}
    up_z = {"gy": gy, "gz": (gz + 1) % 4, "band": band}
    down_z = {"gy": gy, "gz": (gz + 3) % 4, "band": band}
    right, left = ((x + 1) % 4) * 2 + core, ((x + 3) % 4) * 2 + core
    opposite, sibling = ((x + 2) % 4) * 2 + core, x * 2 + 1 - core

    own_at, right_at, left_at, opposite_at = 0, 2, 4, 6
    owners = [band, sibling]
    for chip in (right, left, opposite):
        owners += [chip, chip + 1 - 2 * core]
    load_pan = pltpu.make_async_copy(pan_hbm, gathered.at[pl.ds(0, SHARD)], load_sem.at[0])
    load_cur = pltpu.make_async_copy(cur_hbm, cur, load_sem.at[1])
    load_proj = pltpu.make_async_copy(proj_hbm, proj, load_sem.at[2])
    load_prev = pltpu.make_async_copy(prev_hbm, prev, load_sem.at[3])
    load_pot = pltpu.make_async_copy(pot_hbm, pot, load_sem.at[4])
    for load in (load_pan, load_cur, load_proj, load_prev, load_pot):
        load.start()

    barrier = pltpu.get_barrier_semaphore()
    partners = [at_y((y + r) % 8) for r in range(1, 8)]
    partners += [at_z((z + r) % 8) for r in range(1, 8)]
    partners += [up_y, down_y, up_z, down_z]
    partners += [at_band(right), at_band(left), at_band(sibling)]
    over = (1 - z_hi) * 8
    after_wrap = {"gy": over + (8 - y) % 8, "gz": gz, "band": band}
    before_wrap = {"gy": over + (14 - y) % 8, "gz": gz, "band": band}
    partners += [after_wrap, before_wrap]
    for partner in partners:
        pl.semaphore_signal(barrier, inc=1, device_id=partner, device_id_type=MESH)
    pl.semaphore_wait(barrier, len(partners))

    def remote(source, target, send, recv, device):
        return pltpu.make_async_remote_copy(
            src_ref=source, dst_ref=target, send_sem=send, recv_sem=recv,
            device_id=device, device_id_type=MESH,
        )

    def panel_copy(slot, there, k, size, send, recv, device):
        source = gathered.at[pl.ds(slot * SHARD + k * size, size)]
        target = gathered.at[pl.ds(there * SHARD + k * size, size)]
        return remote(source, target, send, recv, device)

    def to_right(slot, there, k, sems, recvs, at, size=CHUNK):
        return panel_copy(slot, there, k, size, sems.at[at], recvs.at[at], at_band(right))

    def to_left(slot, there, k, sems, recvs, at, size=CHUNK):
        return panel_copy(slot, there, k, size, sems.at[at], recvs.at[at], at_band(left))

    def to_sibling(slot, k, size=CHUNK):
        at = slot // 2 * 4 + k
        return panel_copy(slot, slot + 1, k, size, sib_send.at[at], sib_recv.at[at], at_band(sibling))

    load_pan.wait()
    started = []

    def pass_on(copy):
        copy.start()
        started.append(copy)

    for step in range(4):
        k = step
        pass_on(to_right(own_at, left_at, k, right_send, left_recv, k))
        k = (step + 2) % 4
        pass_on(to_left(own_at, right_at, k, left_send, right_recv, k))
    for k in range(4):
        pass_on(to_sibling(own_at, k))

    load_cur.wait()
    first, rest = pl.ds(0, DIRECT), pl.ds(DIRECT, N - DIRECT)
    upper, lower = pl.ds(16, 48), pl.ds(0, 48)
    halo_y0 = remote(cur.at[first, upper], y_low.at[first], halo_send.at[0], halo_recv.at[0], up_y)
    halo_y1 = remote(cur.at[first, lower], y_high.at[first], halo_send.at[1], halo_recv.at[1], down_y)
    rest_y0 = remote(cur.at[rest, upper], y_low.at[rest], rest_send.at[0], rest_recv.at[0], up_y)
    rest_y1 = remote(cur.at[rest, lower], y_high.at[rest], rest_send.at[1], rest_recv.at[1], down_y)
    around_y0 = remote(cur.at[rest, upper], held, rest_send.at[0], rest_recv.at[2], after_wrap)
    around_y1 = remote(cur.at[rest, lower], held, rest_send.at[1], rest_recv.at[2], before_wrap)
    onward_y0 = remote(held, y_low.at[rest], rest_send.at[2], rest_recv.at[0], down_y)
    onward_y1 = remote(held, y_high.at[rest], rest_send.at[2], rest_recv.at[1], up_y)

    def under(condition, action):
        @pl.when(condition)
        def _():
            action()

    under(y == 7, around_y0.start)
    under(y == 0, around_y1.start)
    under(y != 7, rest_y0.start)
    under(y != 0, rest_y1.start)
    halo_y0.start()
    halo_y1.start()

    @pl.loop(0, N)
    def _(n):
        for layer in range(C):
            turned[n, layer * 8 : layer * 8 + 8, :] = cur[n, pl.ds(layer, 8, stride=8), :]

    halo_z0 = remote(turned.at[:, pl.ds(16, 48)], z_low, halo_send.at[2], halo_recv.at[2], up_z)
    halo_z1 = remote(turned.at[:, pl.ds(0, 48)], z_high, halo_send.at[3], halo_recv.at[3], down_z)
    halo_z0.start()
    halo_z1.start()

    transpose_block(cur, block)
    load_proj.wait()
    convert(proj, proj_split, 0, NPR)
    contract(proj_split, block, sums, 0, NPR)

    lane = lax.broadcasted_iota(jnp.int32, (N, NPR), 1)
    tile = gy * 4 + gz
    weight = jnp.zeros((N, NPR), F32)
    for b in range(8):
        reached = pattern[b, tile].astype(F32)
        live = ((lane >> 3) == b) & ((lane & 7) < counts[b])
        weight = jnp.where(live, reached, weight)
    coupling = jnp.zeros((N, NPR), F32)
    for j in range(NPR):
        coupling = jnp.where(lane == j, coup[j], coupling)

    def send_y(buffer, sems):
        copies = []
        for r in range(1, 8):
            copies.append(
                remote(buffer.at[y], buffer.at[y], sum_send.at[sems, r], sum_recv.at[sems, y], at_y((y + r) % 8))
            )
            copies[-1].start()
        return copies

    def send_z(buffer, sems):
        copies = []
        for r in range(1, 8):
            copies.append(
                remote(buffer.at[z], buffer.at[z], sum_send.at[sems, r], sum_recv.at[sems, z], at_z((z + r) % 8))
            )
            copies[-1].start()
        return copies

    def receive(buffer, sems, me):
        for r in range(1, 8):
            other = (me + r) % 8
            remote(buffer.at[other], buffer.at[other], sum_send.at[sems, r], sum_recv.at[sems, other], up_y).wait_recv()

    def total(buffer):
        value = buffer[0]
        for i in range(1, 8):
            value = value + buffer[i]
        return value

    small_a[y] = pack(fold_layers(sums[0:NPR, :]) * weight)
    sent = send_y(small_a, 0)

    load_prev.wait()
    load_pot.wait()

    @pl.loop(0, N)
    def _(n):
        value = cur[n]
        lap = 3.0 * STENCIL[0] * value
        for reach in range(1, 7):
            lap = lap + STENCIL[reach] * (pltpu.roll(value, reach, 1) + pltpu.roll(value, X - reach, 1))
        filt[n] = SCALE * (-0.5 * lap + pot[...] * value - CENTER * value) - prev[n]

    receive(small_a, 0, y)
    small_b[z] = total(small_a)
    sent += send_z(small_b, 1)

    @pl.loop(0, 6)
    def _(step):
        at = pl.multiple_of(step * 256, 256)
        row = lax.broadcasted_iota(jnp.int32, (NEAR, 256), 0)
        column = lax.broadcasted_iota(jnp.int32, (NEAR, 256), 1) + at
        repeat[:, pl.ds(at, 256)] = jnp.where(row == (column >> 3), 1.0, 0.0).astype(BF16)

    convert(gathered, pan_split, 0, SHARD)

    for step in range(4):
        k = step
        to_right(own_at, left_at, k, right_send, left_recv, k).wait_recv()
        if k < 2:
            for i in (2 * k, 2 * k + 1):
                pass_on(to_right(left_at, opposite_at, i, ahead_send, behind_recv, i, PIECE))
        pass_on(to_sibling(left_at, k))
        k = (step + 2) % 4
        to_left(own_at, right_at, k, left_send, right_recv, k).wait_recv()
        if k >= 2:
            for i in (2 * k, 2 * k + 1):
                pass_on(to_left(right_at, opposite_at, i, back_send, front_recv, i - 4, PIECE))
        pass_on(to_sibling(right_at, k))

    @pl.when(y == 1)
    def _():
        around_y0.wait_recv()
        onward_y0.start()

    @pl.when(y == 6)
    def _():
        around_y1.wait_recv()
        onward_y1.start()

    def take(slot):
        for k in range(4):
            to_sibling(slot, k).wait_recv()

    take(own_at)
    convert(gathered, pan_split, SHARD, SHARD)
    convert(gathered, pan_split, right_at * SHARD, SHARD)
    convert(gathered, pan_split, left_at * SHARD, SHARD)

    receive(small_b, 1, z)
    spread(unpack(total(small_b)) * (coupling * weight), repeat, spread_ref, 0)
    for part in range(4):
        at = part * 256
        value = dot(spread_ref[:, 0:512], proj_split[:, at : at + 256])
        value = value[0:128] + value[128:256] + dot(spread_ref[0:128, 0:512], proj_split[:, 1024 + at : 1280 + at])
        for half in range(2):
            rows = pl.ds((part * 2 + half) * 8, 8)
            filt[:, rows, :] += SCALE * value[:, half * X : (half + 1) * X].reshape(N, 8, X)

    take(right_at)
    convert(gathered, pan_split, (right_at + 1) * SHARD, SHARD)
    take(left_at)
    convert(gathered, pan_split, (left_at + 1) * SHARD, SHARD)

    for copy in (halo_y0, halo_y1, rest_y0, rest_y1):
        copy.wait_recv()

    def stencil(rows):
        result = []
        for at in range(C):
            value = None
            for reach in range(1, 7):
                pair = STENCIL[reach] * (rows[6 + at + reach] + rows[6 + at - reach])
                value = pair if value is None else value + pair
            result.append(-0.5 * SCALE * value)
        return result

    def lines(ref, n, count):
        return [ref[n, i * 8 : i * 8 + 8, :] for i in range(count)]

    @pl.loop(0, N)
    def _(n):
        parts = stencil(lines(y_low, n, 6) + lines(cur, n, 8) + lines(y_high, n, 6))
        for at in range(C):
            filt[n, at * 8 : at * 8 + 8, :] += parts[at]

    halo_z0.wait_recv()
    halo_z1.wait_recv()

    @pl.loop(0, N)
    def _(n):
        parts = stencil(lines(z_low, n, 6) + lines(turned, n, 8) + lines(z_high, n, 6))
        for at in range(C):
            filt[n, pl.ds(at, 8, stride=8), :] += parts[at]

    transpose_block(filt, block)

    contract(pan_split, block, sums, 0, NEAR)
    near = fold_layers(sums[0:NEAR, :])
    near_a[y, 0:16, :] = near[:, 0:128]
    near_a[y, 16:24, :] = pack(near[:, 128:NEAR])
    sent += send_y(near_a, 2)
    for i in range(4):
        to_right(left_at, opposite_at, i, ahead_send, behind_recv, i, PIECE).wait_recv()
        pass_on(to_sibling(opposite_at, i, PIECE))
        to_left(right_at, opposite_at, i + 4, back_send, front_recv, i, PIECE).wait_recv()
        pass_on(to_sibling(opposite_at, i + 4, PIECE))
    convert(gathered, pan_split, opposite_at * SHARD, SHARD)
    contract(pan_split, block, sums, NEAR, SHARD)
    for i in range(8):
        to_sibling(opposite_at, i, PIECE).wait_recv()
    convert(gathered, pan_split, (opposite_at + 1) * SHARD, SHARD)
    contract(pan_split, block, sums, NEAR + SHARD, SHARD)
    far_a[y] = pack(fold_layers(sums[NEAR:NP, :]))
    sent += send_y(far_a, 3)
    receive(near_a, 2, y)
    near_b[z] = total(near_a)
    sent += send_z(near_b, 4)
    receive(far_a, 3, y)
    far_b[z] = total(far_a)
    sent += send_z(far_b, 5)

    def take_away(first, count, part):
        at = part * 256
        table = pl.ds(first * 8, count * 8)
        value = dot(spread_ref[:, table], pan_split[table, at : at + 256])
        value = value[0:128] + value[128:256] + dot(spread_ref[0:128, table], pan_split[table, 1024 + at : 1280 + at])
        for half in range(2):
            rows = pl.ds((part * 2 + half) * 8, 8)
            filt[:, rows, :] -= value[:, half * X : (half + 1) * X].reshape(N, 8, X)

    def write_coefs(coefs, slot):
        values = coefs.T
        for i in range(coefs.shape[1] // SHARD):
            rows = pl.ds(pl.multiple_of(owners[slot + i] * SHARD, SHARD), SHARD)
            coef_rows[rows, :] = values[i * SHARD : (i + 1) * SHARD, :]

    receive(near_b, 4, z)
    packed = total(near_b)
    near = jnp.concatenate([packed[0:16], unpack(packed[16:24])], axis=1)
    spread(near, repeat, spread_ref, 0)
    for part in range(4):
        take_away(0, NEAR, part)
    write_coefs(near, 0)
    receive(far_b, 5, z)
    far = unpack(total(far_b))
    spread(far, repeat, spread_ref, NEAR * 8)
    stores = []
    for part in range(4):
        take_away(NEAR, NP - NEAR, part)
        rows = pl.ds(part * 16, 16)
        stores.append(pltpu.make_async_copy(filt.at[:, rows], out_hbm.at[:, rows], store_sem.at[part]))
        stores[-1].start()
    write_coefs(far, opposite_at)
    coef_out[...] = coef_rows[...].T

    for copy in started + sent + [halo_y0, halo_y1, rest_y0, rest_y1, halo_z0, halo_z1]:
        copy.wait_send()
    under((y == 1) | (y == 6), onward_y0.wait_send)
    for copy in stores:
        copy.wait()


def finish(rotated, coefs, rotated_out, coefs_out):
    rotated_out[...] = rotated[...]
    coefs_out[...] = coefs[...]


def per_device(previous, current, potential, projectors, couplings, pattern, counts, panels):
    rows = C * C
    vmem = pltpu.VMEM
    dma = pltpu.SemaphoreType.DMA
    rotated, coefs = pl.pallas_call(
        kernel,
        out_shape=(
            jax.ShapeDtypeStruct((N, rows, X), F32),
            jax.ShapeDtypeStruct((N, NP), F32),
        ),
        in_specs=[ANY, ANY, ANY, ANY, SMEM, SMEM, SMEM, ANY],
        out_specs=(ANY, pl.BlockSpec(memory_space=pltpu.VMEM)),
        scratch_shapes=[
            vmem((N, rows, X), F32),
            vmem((N, rows, X), F32),
            vmem((N, 48, X), F32),
            vmem((N, 48, X), F32),
            vmem((N, 48, X), F32),
            vmem((N, 48, X), F32),
            vmem((N, rows, X), F32),
            vmem((N, rows, X), F32),
            vmem((rows, X), F32),
            vmem((NPR, rows, X), F32),
            vmem((NPR * 8, 2048), BF16),
            vmem((NP, rows, X), F32),
            vmem((NP * 8, 2048), BF16),
            vmem((1024, 256), BF16),
            vmem((NEAR, 1536), BF16),
            vmem((256, 2048), BF16),
            vmem((NP, 128), F32),
            vmem((8, 8, 128), F32),
            vmem((8, 8, 128), F32),
            vmem((8, 24, 128), F32),
            vmem((8, 24, 128), F32),
            vmem((8, 8, 128), F32),
            vmem((8, 8, 128), F32),
            vmem((N - DIRECT, 48, X), F32),
            vmem((NP, N), F32),
            dma((5,)),
            dma((4,)),
            dma((4,)),
            dma((3,)),
            dma((3,)),
            dma((4,)),
            dma((4,)),
            dma((4,)),
            dma((4,)),
            dma((20,)),
            dma((20,)),
            dma((4,)),
            dma((4,)),
            dma((4,)),
            dma((4,)),
            dma((6, 8)),
            dma((6, 8)),
            dma((4,)),
        ],
        compiler_params=pltpu.CompilerParams(
            collective_id=0, has_side_effects=True, vmem_limit_bytes=56 * 1024 * 1024
        ),
        cost_estimate=pl.CostEstimate(flops=10**9, bytes_accessed=5 * 2**20, transcendentals=0),
        name="filter_step",
    )(
        previous.reshape(N, rows, X),
        current.reshape(N, rows, X),
        potential.reshape(rows, X),
        projectors.reshape(NPR, rows, X),
        couplings,
        pattern,
        counts,
        panels.reshape(SHARD, rows, X),
    )
    rotated, coefs = pl.pallas_call(
        finish,
        out_shape=(
            jax.ShapeDtypeStruct((N, rows, X), F32),
            jax.ShapeDtypeStruct((N, NP), F32),
        ),
        in_specs=[pl.BlockSpec(memory_space=pltpu.VMEM), pl.BlockSpec(memory_space=pltpu.VMEM)],
        out_specs=(pl.BlockSpec(memory_space=pltpu.VMEM), pl.BlockSpec(memory_space=pltpu.VMEM)),
        name="finish",
    )(rotated, coefs)
    return rotated.reshape(N, C, C, X), coefs.T


def solution(mesh):
    in_specs = (
        P("band", "gy", "gz", None),
        P("band", "gy", "gz", None),
        P("gy", "gz", None),
        P(None, "gy", "gz", None),
        P(),
        P(),
        P(),
        P("band", "gy", "gz", None),
    )
    out_specs = (P("band", "gy", "gz", None), P(None, "band"))
    return jax.shard_map(
        per_device, mesh=mesh, in_specs=in_specs, out_specs=out_specs, check_vma=False
    )
```

```python
import jax
import jax.numpy as jnp
from jax import lax
from jax.experimental import pallas as pl
from jax.experimental.pallas import tpu as pltpu
from jax.sharding import PartitionSpec as P

STENCIL = (
    -5369.0 / 1800.0,
    12.0 / 7.0,
    -15.0 / 56.0,
    10.0 / 189.0,
    -1.0 / 112.0,
    2.0 / 1925.0,
    -1.0 / 16632.0,
)
CENTER = 1.0
HALF_WIDTH = 5.0
SCALE = 2.0 / HALF_WIDTH

N = 16
C = 8
X = 128
NPR = 64
SHARD = 32
NP = 256
NEAR = 192
CHUNK = 8
PIECE = 4
DIRECT = 6
ROUND = 5
FAR_FIRST = (4, 3, 5, 2, 6, 1, 7)
F32 = jnp.float32
BF16 = jnp.bfloat16
MESH = pl.DeviceIdType.MESH
ANY = pl.BlockSpec(memory_space=pl.ANY)
SMEM = pl.BlockSpec(memory_space=pltpu.SMEM)


def split(value):
    high = value.astype(BF16)
    return high, (value - high.astype(F32)).astype(BF16)


def same_layer(rows, columns):
    row = lax.broadcasted_iota(jnp.int32, (rows, columns), 0)
    column = lax.broadcasted_iota(jnp.int32, (rows, columns), 1)
    return (row & 7) == (column & 7)


def dot(left, right):
    return jnp.dot(left, right, preferred_element_type=F32)


def convert(source, target, first, count):
    @pl.loop(0, count // 16)
    def _(step):
        start = pl.multiple_of(first + step * 16, 8)
        row = pl.multiple_of(start * 8, 64)
        for y in range(C):
            rows = source[pl.ds(start, 16), y * 8 : y * 8 + 8, :].reshape(128, X)
            high, low = split(rows)
            target[pl.ds(row, 128), y * X : (y + 1) * X] = high
            target[pl.ds(row, 128), (C + y) * X : (C + y + 1) * X] = low


def transpose_block(source, target):
    for y in range(C):
        rows = source[:, y * 8 : y * 8 + 8, :].reshape(N * 8, X).T
        high, low = split(rows)
        target[y * X : (y + 1) * X, 0:128] = high
        target[y * X : (y + 1) * X, 128:256] = low


def contract(table, block, sums, first, count, shift=0):
    @pl.loop(0, count // 32)
    def _(step):
        start = pl.multiple_of(first + step * 32, 32)
        rows = pl.ds(pl.multiple_of(start * 8, 256), 256)
        full = dot(table[rows, 0:1024], block[...]) + dot(table[rows, 1024:2048], block[...])
        both = full[:, 0:128] + full[:, 128:256]
        kept = jnp.where(same_layer(256, 128), both, 0.0)
        sums[pl.ds(start + shift, 32), :] = kept.reshape(32, 8, 128).sum(axis=1)


def fold_layers(sums):
    band = lax.broadcasted_iota(jnp.int32, (N, 128), 0)
    column = lax.broadcasted_iota(jnp.int32, (N, 128), 1)
    ones = jnp.where(band == (column >> 3), 1.0, 0.0).astype(F32)
    return lax.dot_general(
        ones,
        sums,
        (((1,), (1,)), ((), ())),
        precision=lax.Precision.HIGHEST,
        preferred_element_type=F32,
    )


def pack(coefs):
    return jnp.concatenate([coefs[0:8], coefs[8:16]], axis=1)


def unpack(packed):
    return jnp.concatenate([packed[:, 0:64], packed[:, 64:128]], axis=0)


def spread(coefs, repeat, target, first):
    count = coefs.shape[1]
    columns = count * 8
    wide = jnp.broadcast_to(coefs[:, None, :], (N, 8, count)).reshape(N * 8, count)
    high, low = split(wide)
    both = jnp.concatenate([high, low], axis=0)
    for at in range(0, columns, 256):
        values = dot(both, repeat[0:count, at : at + 256])
        target[:, first + at : first + at + 256] = jnp.where(same_layer(256, 256), values, 0.0).astype(BF16)


def kernel(
    prev_hbm, cur_hbm, pot_hbm, proj_hbm, coup, pattern, counts, pan_hbm,
    out_hbm, coef_out,
    cur, turned, y_low, y_high, z_low, z_high, filt, prev, pot, proj, proj_split,
    gathered, pan_split, block, repeat, spread_ref, sums, small_a, small_b, near_a, near_b, far_a, far_b, held, coef_rows, far_c, other_filt, other_block,
    load_sem, halo_send, halo_recv, rest_send, rest_recv, right_send, left_recv, left_send, right_recv,
    sib_send, sib_recv, ahead_send, behind_recv, back_send, front_recv,
    sum_send, sum_recv, store_sem, mirror_sem,
):
    gy, gz, band = lax.axis_index("gy"), lax.axis_index("gz"), lax.axis_index("band")
    z_hi, y = gy // 8, gy % 8
    z = z_hi * 4 + gz
    x, core = band // 2, band % 2

    def at_y(other):
        return {"gy": z_hi * 8 + other, "gz": gz, "band": band}

    def at_z(other):
        return {"gy": (other // 4) * 8 + y, "gz": other % 4, "band": band}

    def at_band(other):
        return {"gy": gy, "gz": gz, "band": other}

    up_y = {"gy": (gy + 1) % 16, "gz": gz, "band": band}
    down_y = {"gy": (gy + 15) % 16, "gz": gz, "band": band}
    up_z = {"gy": gy, "gz": (gz + 1) % 4, "band": band}
    down_z = {"gy": gy, "gz": (gz + 3) % 4, "band": band}
    right, left = ((x + 1) % 4) * 2 + core, ((x + 3) % 4) * 2 + core
    opposite, sibling = ((x + 2) % 4) * 2 + core, x * 2 + 1 - core

    def at_other_core(other):
        return {"gy": (other // 4) * 8 + y, "gz": other % 4, "band": sibling}

    own_at, right_at, left_at, opposite_at = 0, 2, 4, 6
    owners = [band, sibling]
    for chip in (right, left, opposite):
        owners += [chip, chip + 1 - 2 * core]
    load_pan = pltpu.make_async_copy(pan_hbm, gathered.at[pl.ds(0, SHARD)], load_sem.at[0])
    load_cur = pltpu.make_async_copy(cur_hbm, cur, load_sem.at[1])
    load_proj = pltpu.make_async_copy(proj_hbm, proj, load_sem.at[2])
    load_prev = pltpu.make_async_copy(prev_hbm, prev, load_sem.at[3])
    load_pot = pltpu.make_async_copy(pot_hbm, pot, load_sem.at[4])
    for load in (load_pan, load_cur, load_proj, load_prev, load_pot):
        load.start()

    barrier = pltpu.get_barrier_semaphore()
    partners = [at_y((y + r) % 8) for r in FAR_FIRST]
    partners += [at_z((z + r) % 8) for r in FAR_FIRST]
    partners += [at_band(right), at_band(left), at_band(sibling)]
    partners += [at_other_core((z + r) % 8) for r in FAR_FIRST]
    over = (1 - z_hi) * 8
    after_wrap = {"gy": over + (8 - y) % 8, "gz": gz, "band": band}
    before_wrap = {"gy": over + (14 - y) % 8, "gz": gz, "band": band}
    across = {"gy": over + 7 - y, "gz": gz, "band": band}
    after_next = {"gy": over + (9 - y) % 8, "gz": gz, "band": band}
    before_next = {"gy": over + (13 - y) % 8, "gz": gz, "band": band}
    partners = [after_wrap, before_wrap, after_next, before_next, across] + partners
    for partner in partners:
        pl.semaphore_signal(barrier, inc=1, device_id=partner, device_id_type=MESH)
    pl.semaphore_wait(barrier, len(partners))

    def remote(source, target, send, recv, device):
        return pltpu.make_async_remote_copy(
            src_ref=source, dst_ref=target, send_sem=send, recv_sem=recv,
            device_id=device, device_id_type=MESH,
        )

    def panel_copy(slot, there, k, size, send, recv, device):
        source = gathered.at[pl.ds(slot * SHARD + k * size, size)]
        target = gathered.at[pl.ds(there * SHARD + k * size, size)]
        return remote(source, target, send, recv, device)

    def to_right(slot, there, k, sems, recvs, at, size=CHUNK):
        return panel_copy(slot, there, k, size, sems.at[at], recvs.at[at], at_band(right))

    def to_left(slot, there, k, sems, recvs, at, size=CHUNK):
        return panel_copy(slot, there, k, size, sems.at[at], recvs.at[at], at_band(left))

    def to_sibling(slot, k, size=CHUNK):
        at = slot // 2 * 4 + k
        return panel_copy(slot, slot + 1, k, size, sib_send.at[at], sib_recv.at[at], at_band(sibling))

    load_pan.wait()
    started = []

    def pass_on(copy):
        copy.start()
        started.append(copy)

    def send_own(steps):
        for step in steps:
            pass_on(to_right(own_at, left_at, step, right_send, left_recv, step))
            k = (step + 2) % 4
            pass_on(to_left(own_at, right_at, k, left_send, right_recv, k))

    send_own((0, 1))
    for k in range(4):
        pass_on(to_sibling(own_at, k))

    load_cur.wait()
    first = pl.ds(0, DIRECT)
    upper, lower = pl.ds(16, 48), pl.ds(0, 48)
    halo_y0 = remote(cur.at[first, upper], y_low.at[first], halo_send.at[0], halo_recv.at[0], up_y)
    halo_y1 = remote(cur.at[first, lower], y_high.at[first], halo_send.at[1], halo_recv.at[1], down_y)

    def under(condition, action):
        @pl.when(condition)
        def _():
            action()

    plain, around, onward = [], [], []
    for i, (after, before) in enumerate(((after_wrap, before_wrap), (after_next, before_next))):
        rest = pl.ds(DIRECT + i * ROUND, ROUND)
        s0, s1, s2 = (rest_send.at[k * 2 + i] for k in range(3))
        r0, r1, r2 = (rest_recv.at[k * 2 + i] for k in range(3))
        plain.append(remote(cur.at[rest, upper], y_low.at[rest], s0, r0, up_y))
        plain.append(remote(cur.at[rest, lower], y_high.at[rest], s1, r1, down_y))
        around.append(remote(cur.at[rest, upper], held, s0, r2, after))
        around.append(remote(cur.at[rest, lower], held, s1, r2, before))
        onward.append(remote(held, y_low.at[rest], s2, r0, at_y(0)))
        onward.append(remote(held, y_high.at[rest], s2, r1, at_y(7)))
    for i in range(4):
        edge = 7 if i % 2 == 0 else 0
        under(y == edge, around[i].start)
        under(y != edge, plain[i].start)
    halo_y0.start()
    halo_y1.start()

    @pl.loop(0, N)
    def _(n):
        for layer in range(C):
            turned[n, layer * 8 : layer * 8 + 8, :] = cur[n, pl.ds(layer, 8, stride=8), :]

    halo_z0 = remote(turned.at[:, pl.ds(16, 48)], z_low, halo_send.at[2], halo_recv.at[2], up_z)
    halo_z1 = remote(turned.at[:, pl.ds(0, 48)], z_high, halo_send.at[3], halo_recv.at[3], down_z)
    halo_z0.start()
    halo_z1.start()

    transpose_block(cur, block)
    load_proj.wait()
    convert(proj, proj_split, 0, NPR)
    contract(proj_split, block, sums, 0, NPR)

    lane = lax.broadcasted_iota(jnp.int32, (N, NPR), 1)
    tile = gy * 4 + gz
    weight = jnp.zeros((N, NPR), F32)
    for b in range(8):
        reached = pattern[b, tile].astype(F32)
        live = ((lane >> 3) == b) & ((lane & 7) < counts[b])
        weight = jnp.where(live, reached, weight)
    coupling = jnp.zeros((N, NPR), F32)
    for j in range(NPR):
        coupling = jnp.where(lane == j, coup[j], coupling)

    def send_y(buffer, sems):
        copies = []
        for r in FAR_FIRST:
            copies.append(
                remote(buffer.at[y], buffer.at[y], sum_send.at[sems, r], sum_recv.at[sems, y], at_y((y + r) % 8))
            )
            copies[-1].start()
        return copies

    def send_z(buffer, sems):
        copies = []
        for r in FAR_FIRST:
            copies.append(
                remote(buffer.at[z], buffer.at[z], sum_send.at[sems, r], sum_recv.at[sems, z], at_z((z + r) % 8))
            )
            copies[-1].start()
        return copies

    def receive(buffer, sems, me):
        for r in range(1, 8):
            other = (me + r) % 8
            remote(buffer.at[other], buffer.at[other], sum_send.at[sems, r], sum_recv.at[sems, other], up_y).wait_recv()

    def total(buffer):
        value = buffer[0]
        for i in range(1, 8):
            value = value + buffer[i]
        return value

    small_a[y] = pack(fold_layers(sums[0:NPR, :]) * weight)
    sent = send_y(small_a, 0)

    load_prev.wait()
    load_pot.wait()

    @pl.loop(0, N)
    def _(n):
        value = cur[n]
        lap = 3.0 * STENCIL[0] * value
        for reach in range(1, 7):
            lap = lap + STENCIL[reach] * (pltpu.roll(value, reach, 1) + pltpu.roll(value, X - reach, 1))
        filt[n] = SCALE * (-0.5 * lap + pot[...] * value - CENTER * value) - prev[n]

    send_own((2, 3))

    receive(small_a, 0, y)
    small_b[z] = total(small_a)
    sent += send_z(small_b, 1)

    @pl.loop(0, 6)
    def _(step):
        at = pl.multiple_of(step * 256, 256)
        row = lax.broadcasted_iota(jnp.int32, (NEAR, 256), 0)
        column = lax.broadcasted_iota(jnp.int32, (NEAR, 256), 1) + at
        repeat[:, pl.ds(at, 256)] = jnp.where(row == (column >> 3), 1.0, 0.0).astype(BF16)

    convert(gathered, pan_split, 0, SHARD)

    for step in range(4):
        k = step
        to_right(own_at, left_at, k, right_send, left_recv, k).wait_recv()
        if k < 2:
            for i in (2 * k, 2 * k + 1):
                pass_on(to_right(left_at, opposite_at, i, ahead_send, behind_recv, i, PIECE))
        pass_on(to_sibling(left_at, k))
        k = (step + 2) % 4
        to_left(own_at, right_at, k, left_send, right_recv, k).wait_recv()
        if k >= 2:
            for i in (2 * k, 2 * k + 1):
                pass_on(to_left(right_at, opposite_at, i, back_send, front_recv, i - 4, PIECE))
        pass_on(to_sibling(right_at, k))

    def hand_on(i):
        around[i].wait_recv()
        onward[i].start()

    holders = (1, 6, 2, 5)
    for i in range(4):
        under(y == holders[i], lambda i=i: hand_on(i))

    def take(slot):
        for k in range(4):
            to_sibling(slot, k).wait_recv()

    take(own_at)
    convert(gathered, pan_split, SHARD, SHARD)
    convert(gathered, pan_split, right_at * SHARD, SHARD)
    convert(gathered, pan_split, left_at * SHARD, SHARD)

    receive(small_b, 1, z)
    spread(unpack(total(small_b)) * (coupling * weight), repeat, spread_ref, 0)
    for part in range(4):
        at = part * 256
        value = dot(spread_ref[:, 0:512], proj_split[:, at : at + 256])
        value = value[0:128] + value[128:256] + dot(spread_ref[0:128, 0:512], proj_split[:, 1024 + at : 1280 + at])
        for half in range(2):
            rows = pl.ds((part * 2 + half) * 8, 8)
            filt[:, rows, :] += SCALE * value[:, half * X : (half + 1) * X].reshape(N, 8, X)

    for copy in [halo_y0, halo_y1] + plain:
        copy.wait_recv()

    def stencil(rows):
        result = []
        for at in range(C):
            value = None
            for reach in range(1, 7):
                pair = STENCIL[reach] * (rows[6 + at + reach] + rows[6 + at - reach])
                value = pair if value is None else value + pair
            result.append(-0.5 * SCALE * value)
        return result

    def lines(ref, n, count):
        return [ref[n, i * 8 : i * 8 + 8, :] for i in range(count)]

    @pl.loop(0, N)
    def _(n):
        parts = stencil(lines(y_low, n, 6) + lines(cur, n, 8) + lines(y_high, n, 6))
        for at in range(C):
            filt[n, at * 8 : at * 8 + 8, :] += parts[at]

    halo_z0.wait_recv()
    halo_z1.wait_recv()

    @pl.loop(0, N)
    def _(n):
        parts = stencil(lines(z_low, n, 6) + lines(turned, n, 8) + lines(z_high, n, 6))
        for at in range(C):
            filt[n, pl.ds(at, 8, stride=8), :] += parts[at]

    mirror = remote(filt, other_filt, mirror_sem.at[0], mirror_sem.at[1], at_band(sibling))
    mirror.start()
    transpose_block(filt, block)

    contract(pan_split, block, sums, 0, (right_at + 1) * SHARD)
    contract(pan_split, block, sums, left_at * SHARD, SHARD)
    for slot in (right_at, left_at):
        take(slot)
        convert(gathered, pan_split, (slot + 1) * SHARD, SHARD)
        contract(pan_split, block, sums, (slot + 1) * SHARD, SHARD)
    near = fold_layers(sums[0:NEAR, :])
    near_a[y, 0:16, :] = near[:, 0:128]
    near_a[y, 16:24, :] = pack(near[:, 128:NEAR])
    sent += send_y(near_a, 2)
    mirror.wait_recv()
    transpose_block(other_filt, other_block)

    for i in range(4):
        to_right(left_at, opposite_at, i, ahead_send, behind_recv, i, PIECE).wait_recv()
        pass_on(to_sibling(opposite_at, i, PIECE))
        to_left(right_at, opposite_at, i + 4, back_send, front_recv, i, PIECE).wait_recv()
        pass_on(to_sibling(opposite_at, i + 4, PIECE))
    convert(gathered, pan_split, opposite_at * SHARD, SHARD)
    contract(pan_split, block, sums, NEAR, SHARD)
    contract(pan_split, other_block, sums, NEAR, SHARD, SHARD)
    far_a[y] = pack(fold_layers(sums[NEAR:NP, :]))
    sent += send_y(far_a, 3)
    receive(near_a, 2, y)
    near_b[z] = total(near_a)
    sent += send_z(near_b, 4)
    for i in range(8):
        to_sibling(opposite_at, i, PIECE).wait_recv()
    convert(gathered, pan_split, (opposite_at + 1) * SHARD, SHARD)
    receive(far_a, 3, y)
    far_b[z] = total(far_a)
    sent += send_z(far_b, 5)
    for r in (4, 3, 5, 2, 6, 1, 7, 0):
        other = at_other_core((z + r) % 8)
        sent.append(remote(far_b.at[z], far_c.at[z], sum_send.at[6, r], sum_recv.at[6, z], other))
        sent[-1].start()

    def take_away(first, count, part):
        at = part * 256
        table = pl.ds(first * 8, count * 8)
        value = dot(spread_ref[:, table], pan_split[table, at : at + 256])
        value = value[0:128] + value[128:256] + dot(spread_ref[0:128, table], pan_split[table, 1024 + at : 1280 + at])
        for half in range(2):
            rows = pl.ds((part * 2 + half) * 8, 8)
            filt[:, rows, :] -= value[:, half * X : (half + 1) * X].reshape(N, 8, X)

    def write_coefs(coefs, slot):
        values = coefs.T
        for i in range(coefs.shape[1] // SHARD):
            rows = pl.ds(pl.multiple_of(owners[slot + i] * SHARD, SHARD), SHARD)
            coef_rows[rows, :] = values[i * SHARD : (i + 1) * SHARD, :]

    receive(near_b, 4, z)
    packed = total(near_b)
    near = jnp.concatenate([packed[0:16], unpack(packed[16:24])], axis=1)
    spread(near, repeat, spread_ref, 0)
    mirror.wait_send()
    for part in range(4):
        take_away(0, NEAR, part)
    write_coefs(near, 0)
    receive(far_b, 5, z)
    for r in range(8):
        other = (z + r) % 8
        remote(
            far_c.at[other], far_c.at[other], sum_send.at[6, r], sum_recv.at[6, other], at_band(sibling)
        ).wait_recv()
    far = jnp.concatenate([unpack(total(far_b))[:, 0:SHARD], unpack(total(far_c))[:, SHARD : 2 * SHARD]], axis=1)
    spread(far, repeat, spread_ref, NEAR * 8)
    stores = []
    for part in range(4):
        take_away(NEAR, NP - NEAR, part)
        rows = pl.ds(part * 16, 16)
        stores.append(pltpu.make_async_copy(filt.at[:, rows], out_hbm.at[:, rows], store_sem.at[part]))
        stores[-1].start()
    write_coefs(far, opposite_at)
    coef_out[...] = coef_rows[...].T

    for copy in started + sent + [halo_y0, halo_y1, halo_z0, halo_z1] + plain:
        copy.wait_send()
    for i in range(4):
        under(y == holders[i], onward[i].wait_send)
    for copy in stores:
        copy.wait()


def finish(rotated, coefs, rotated_out, coefs_out):
    rotated_out[...] = rotated[...]
    coefs_out[...] = coefs[...]


def per_device(previous, current, potential, projectors, couplings, pattern, counts, panels):
    rows = C * C
    vmem = pltpu.VMEM
    dma = pltpu.SemaphoreType.DMA
    rotated, coefs = pl.pallas_call(
        kernel,
        out_shape=(
            jax.ShapeDtypeStruct((N, rows, X), F32),
            jax.ShapeDtypeStruct((N, NP), F32),
        ),
        in_specs=[ANY, ANY, ANY, ANY, SMEM, SMEM, SMEM, ANY],
        out_specs=(ANY, pl.BlockSpec(memory_space=pltpu.VMEM)),
        scratch_shapes=[
            vmem((N, rows, X), F32),
            vmem((N, rows, X), F32),
            vmem((N, 48, X), F32),
            vmem((N, 48, X), F32),
            vmem((N, 48, X), F32),
            vmem((N, 48, X), F32),
            vmem((N, rows, X), F32),
            vmem((N, rows, X), F32),
            vmem((rows, X), F32),
            vmem((NPR, rows, X), F32),
            vmem((NPR * 8, 2048), BF16),
            vmem((NP, rows, X), F32),
            vmem((NP * 8, 2048), BF16),
            vmem((1024, 256), BF16),
            vmem((NEAR, 1536), BF16),
            vmem((256, 2048), BF16),
            vmem((NP, 128), F32),
            vmem((8, 8, 128), F32),
            vmem((8, 8, 128), F32),
            vmem((8, 24, 128), F32),
            vmem((8, 24, 128), F32),
            vmem((8, 8, 128), F32),
            vmem((8, 8, 128), F32),
            vmem((ROUND, 48, X), F32),
            vmem((NP, N), F32),
            vmem((8, 8, 128), F32),
            vmem((N, rows, X), F32),
            vmem((1024, 256), BF16),
            dma((5,)),
            dma((4,)),
            dma((4,)),
            dma((6,)),
            dma((6,)),
            dma((4,)),
            dma((4,)),
            dma((4,)),
            dma((4,)),
            dma((20,)),
            dma((20,)),
            dma((4,)),
            dma((4,)),
            dma((4,)),
            dma((4,)),
            dma((7, 8)),
            dma((7, 8)),
            dma((4,)),
            dma((2,)),
        ],
        compiler_params=pltpu.CompilerParams(
            collective_id=0, has_side_effects=True, vmem_limit_bytes=56 * 1024 * 1024
        ),
        cost_estimate=pl.CostEstimate(flops=10**9, bytes_accessed=5 * 2**20, transcendentals=0),
        name="filter_step",
    )(
        previous.reshape(N, rows, X),
        current.reshape(N, rows, X),
        potential.reshape(rows, X),
        projectors.reshape(NPR, rows, X),
        couplings,
        pattern,
        counts,
        panels.reshape(SHARD, rows, X),
    )
    rotated, coefs = pl.pallas_call(
        finish,
        out_shape=(
            jax.ShapeDtypeStruct((N, rows, X), F32),
            jax.ShapeDtypeStruct((N, NP), F32),
        ),
        in_specs=[pl.BlockSpec(memory_space=pltpu.VMEM), pl.BlockSpec(memory_space=pltpu.VMEM)],
        out_specs=(pl.BlockSpec(memory_space=pltpu.VMEM), pl.BlockSpec(memory_space=pltpu.VMEM)),
        name="finish",
    )(rotated, coefs)
    return rotated.reshape(N, C, C, X), coefs.T


def solution(mesh):
    in_specs = (
        P("band", "gy", "gz", None),
        P("band", "gy", "gz", None),
        P("gy", "gz", None),
        P(None, "gy", "gz", None),
        P(),
        P(),
        P(),
        P("band", "gy", "gz", None),
    )
    out_specs = (P("band", "gy", "gz", None), P(None, "band"))
    return jax.shard_map(
        per_device, mesh=mesh, in_specs=in_specs, out_specs=out_specs, check_vma=False
    )
```
